32 devices in a mesh: dp: 8 (over z, core), proto: 4 (over y, x).
Axes of the slice: x: 2, y: 2, z: 4, core: 2. Of those that a mesh axis runs over, the one named last changes fastest.
Arguments:
- codes_view: bfloat16 [4096, 256], P('dp'), may hold values from -16 to 16
- pred_view: bfloat16 [4096, 256], P('dp'), may hold values from -32 to 32
- prototypes: bfloat16 [65536, 256], P(('proto', 'dp')), may hold values from -1.5 to 1.5
Outputs:
- swap_loss: float32 [4096], P('dp')
- pull: float32 [4096, 256], P('dp', 'proto')
The draws below stay inside these ranges and needn't reach their ends.
All inputs are finite; a program needn't handle non-finite values.
Results may differ from the reference program's by a relative error of at most 0.0025.
Values may be sent and summed in bfloat16 or wider, within the bound.
No kernel may reach another device: no remote copies, remote signals or barrier semaphores. Data moves between devices by JAX's collectives and lax.ppermute only.
A program may use at most 64 MiB of HBM per device.

```python
import math
import jax
import jax.numpy as jnp
from jax import lax

DIM = 256
PROTOS = 65536
ROWS = 4096


def proto_base(key):
    normal_key, scale_key = jax.random.split(key)
    entries = jax.random.normal(normal_key, (PROTOS, DIM), jnp.float32) / math.sqrt(DIM)
    scales = jnp.exp(jax.random.uniform(scale_key, (PROTOS, 1), jnp.float32, math.log(0.3), math.log(3.0)))
    return jnp.clip(entries * scales, -1.5, 1.5)


def drawn_rows(key, spread):
    noise_key, scale_key = jax.random.split(key)
    noise = jax.random.normal(noise_key, (ROWS, DIM), jnp.float32) * spread
    scales = jnp.exp(jax.random.uniform(scale_key, (ROWS, 1), jnp.float32, math.log(0.3), math.log(3.0)))
    return noise * scales


def draw_prototypes(key, part):
    base = proto_base(key)
    return jnp.clip(base, -1.5, 1.5).astype(jnp.bfloat16)


def draw_codes_view(key, part):
    key = jax.random.fold_in(key, 23)
    values = drawn_rows(key, 0.1)
    return jnp.clip(values, -16.0, 16.0).astype(jnp.bfloat16)


def draw_pred_view(key, part):
    key = jax.random.fold_in(key, 37)
    values = drawn_rows(key, 0.1)
    return jnp.clip(values, -32.0, 32.0).astype(jnp.bfloat16)


def setup_inputs(seed: int = 0) -> dict:
    seeds = jax.random.split(jax.random.key(seed), 4)
    codes_view = draw_codes_view(jax.random.fold_in(seeds[3], 71), 0)
    pred_view = draw_pred_view(jax.random.fold_in(seeds[3], 71), 0)
    prototypes = draw_prototypes(jax.random.fold_in(seeds[3], 71), 0)
    return dict(codes_view=codes_view, pred_view=pred_view, prototypes=prototypes)


code_temp = 0.05
pred_temp = 0.1


def scores(embeds, protos, temp):
    return lax.dot_general(embeds, protos, (((1,), (1,)), ((), ())), preferred_element_type=jnp.float32) / temp


def reference(codes_view, pred_view, prototypes):
    width = min(4096, PROTOS)
    block_count = PROTOS // width
    blocks = prototypes.reshape(block_count, width, DIM)
    total_rows = codes_view.shape[0]

    def column_offset(piece):
        logits = scores(codes_view, piece, code_temp)
        peak = jnp.max(logits, axis=0)
        return peak + jnp.log(jnp.sum(jnp.exp(logits - peak[None, :]), axis=0))

    offsets = lax.map(column_offset, blocks)

    def row_step(carry, inputs):
        piece, offset = inputs
        mass, peak, total = carry
        logits = scores(codes_view, piece, code_temp)
        mass = mass + jnp.sum(jnp.exp(logits - offset[None, :]), axis=1)
        pred = scores(pred_view, piece, pred_temp)
        new_peak = jnp.maximum(peak, jnp.max(pred, axis=1))
        total = total * jnp.exp(peak - new_peak) + jnp.sum(jnp.exp(pred - new_peak[:, None]), axis=1)
        return (mass, new_peak, total), None

    start = (jnp.zeros((total_rows,), jnp.float32), jnp.full((total_rows,), -1e30, jnp.float32), jnp.zeros((total_rows,), jnp.float32))
    (mass, peak, total), _ = lax.scan(row_step, start, (blocks, offsets))
    log_norm = peak + jnp.log(total)

    def target_step(carry, inputs):
        piece, offset = inputs
        cross, pull = carry
        logits = scores(codes_view, piece, code_temp)
        targets = jnp.exp(logits - offset[None, :]) / mass[:, None]
        pred = scores(pred_view, piece, pred_temp)
        probs = jnp.exp(pred - log_norm[:, None])
        cross = cross + jnp.sum(targets * pred, axis=1)
        diff = (targets - probs).astype(jnp.bfloat16)
        pull = pull + jnp.dot(diff, piece, preferred_element_type=jnp.float32)
        return (cross, pull), None

    start = (jnp.zeros((total_rows,), jnp.float32), jnp.zeros((total_rows, DIM), jnp.float32))
    (cross, pull), _ = lax.scan(target_step, start, (blocks, offsets))
    return log_norm - cross, pull
```

```python
import functools
import math

import jax
import jax.numpy as jnp
from jax import lax
from jax.experimental import pallas as pl
from jax.experimental.pallas import tpu as pltpu
from jax.sharding import PartitionSpec as P

code_temp = 0.05
pred_temp = 0.1
code_scale = math.log2(math.e) / code_temp
pred_scale = math.log2(math.e) / pred_temp
log2 = math.log(2.0)
stat_rows = 8
sent_rows = 16
low = -1e30
chunk = 512
kernel_bytes = 24 * 1024 * 1024


def scores(embeds, protos):
    return lax.dot_general(
        embeds, protos, (((1,), (1,)), ((), ())), preferred_element_type=jnp.float32
    )


def bare(value):
    return value.astype(jnp.bfloat16)


def add(parts):
    return functools.reduce(jnp.add, parts)


def lane_fold(combine, value):
    parts = [value[:, i : i + 128] for i in range(0, value.shape[1], 128)]
    return functools.reduce(combine, parts)


def padded(rows, width):
    filler = jnp.zeros((stat_rows - len(rows), width), jnp.float32)
    return jnp.concatenate([*rows, filler], axis=0)


def split_stats(stats):
    terms = []
    for row in stats:
        for _ in range(3):
            term = bare(row)
            row = row - term.astype(jnp.float32)
            terms.append(term)
    filler = jnp.zeros((sent_rows - len(terms), stats[0].shape[1]), jnp.bfloat16)
    return jnp.concatenate([*terms, filler], axis=0)


def join_stats(terms, count):
    wide = terms.astype(jnp.float32)
    return [add([wide[3 * i + j : 3 * i + j + 1] for j in range(3)]) for i in range(count)]


def parted(value):
    share = value.shape[0] - stat_rows
    return value[:share, :], [value[share + i : share + i + 1, :] for i in range(2)]


def parted_sent(value):
    share = value.shape[0] - sent_rows
    return value[:share, :].astype(jnp.float32), join_stats(value[share:, :], 2)


def packed(part):
    pull, stats = part
    return jnp.concatenate([pull, padded(stats, pull.shape[1])], axis=0)


def join_preds(parts):
    peak = functools.reduce(jnp.maximum, [stats[0] for _, stats in parts])
    factors = [jnp.exp2(stats[0] - peak) for _, stats in parts]
    pull = add([part * factor for (part, _), factor in zip(parts, factors)])
    total = add([stats[1] * factor for (_, stats), factor in zip(parts, factors)])
    return pull, [peak, total]


def join_targets(parts):
    stats = [add([stats[i] for _, stats in parts]) for i in range(2)]
    return add([part for part, _ in parts]), stats


joins = {"pred": join_preds, "target": join_targets}


def send(info, place, pull, stats, kept, *sent):
    *sent, flipped = sent
    whole = len(sent) == 1
    count = sent[0].shape[0] if whole else len(sent) + 1
    share = pull.shape[1] // count
    high, tall = share + stat_rows, share + sent_rows
    flipped[...] = pull.T
    mine = pl.multiple_of(info[1] * share, share)
    kept[place * high : place * high + share, :] = flipped[pl.ds(mine, share), :]
    kept[place * high + share : (place + 1) * high, :] = padded(stats, pull.shape[0])
    terms = split_stats(stats)
    for s in range(count) if whole else range(1, count):
        out, start = sent[0].at[s] if whole else sent[s - 1], s * share
        if not whole:
            start = pl.multiple_of((info[1] ^ s) * share, share)
        out[place * tall : place * tall + share, :] = bare(flipped[pl.ds(start, share), :])
        out[place * tall + share : (place + 1) * tall, :] = terms


def whole(value):
    return pl.BlockSpec(value.shape, lambda *_: (0,) * len(value.shape))


def call(kernel, name, info, grid, ins, in_specs, outs, out_specs, scratch, flops, exps):
    values = pl.pallas_call(
        kernel,
        grid_spec=pltpu.PrefetchScalarGridSpec(
            num_scalar_prefetch=1,
            grid=grid,
            in_specs=in_specs,
            out_specs=out_specs,
            scratch_shapes=scratch,
        ),
        out_shape=outs,
        compiler_params=pltpu.CompilerParams(
            vmem_limit_bytes=kernel_bytes if exps else kernel_bytes // 2
        ),
        cost_estimate=pl.CostEstimate(flops=flops, bytes_accessed=flops // 128, transcendentals=exps),
        name=name,
    )(info, *ins)
    info, first = lax.optimization_barrier((info, values[0]))
    return info, first, *values[1:]


def placed_rows(info, quarters, block):
    part = quarters[0].shape[1]
    for s, quarter in enumerate(quarters):
        place = pl.multiple_of((info[1] ^ s) * part, part)
        block[pl.ds(place, part), :] = quarter[0]


def over_chunks(protos, width, step, unrolled=False):
    count = protos[0].shape[0] // width
    if unrolled:
        for i in range(count):
            for half, part in enumerate(protos):
                step(half * count + i, part[i * width : (i + 1) * width, :])
        return

    def both(i, carry):
        at = pl.ds(pl.multiple_of(i * width, width), width)
        for half, part in enumerate(protos):
            step(half * count + i, part[at, :])
        return carry

    lax.fori_loop(0, count, both, 0)


def stats_kernel(fresh, info, *refs):
    if fresh:
        block, *protos, stats = refs
    else:
        *codes, near, across, before, stats, block = refs
        protos = near, across
        placed_rows(info, codes, block)

    @pl.when(pl.program_id(0) == 0)
    def _():
        if fresh:
            stats[:, 0:1, :] = jnp.full((stats.shape[0], 1, stats.shape[2]), low, jnp.float32)
            stats[:, 1:, :] = jnp.zeros((stats.shape[0], stat_rows - 1, stats.shape[2]), jnp.float32)
        else:
            stats[...] = before[...]

    def step(j, protos):
        raw = scores(block[...], protos)
        old, total = stats[j, 0:1, :], stats[j, 1:2, :]
        new = jnp.maximum(old, jnp.max(raw, axis=0, keepdims=True))
        value = jnp.exp2((raw - new) * code_scale)
        stats[j, 1:2, :] = total * jnp.exp2((old - new) * code_scale) + jnp.sum(
            value, axis=0, keepdims=True
        )
        stats[j, 0:1, :] = new

    over_chunks(protos, stats.shape[2], step, True)


def stats_part(info, codes, protos, before, rows):
    count, dim = protos[0].shape
    width = min(chunk, count)
    fresh = before is None
    ins = [*codes, *protos]
    if fresh:
        blocks, scratch = 1, []
        specs = [whole(value) for value in ins]
    else:
        blocks, scratch = codes[0].shape[0], [pltpu.VMEM((rows, dim), jnp.bfloat16)]
        ins = [*ins, before]
        specs = [pl.BlockSpec((1, *part.shape[1:]), lambda i, info: (i, 0, 0)) for part in codes]
        specs += [whole(value) for value in ins[-3:]]
    out = jax.ShapeDtypeStruct((2 * count // width, stat_rows, width), jnp.float32)
    return call(
        functools.partial(stats_kernel, fresh), "stats_part", info, (blocks,), ins, specs, [out],
        [whole(out)], scratch, 4 * blocks * rows * count * dim, 2 * blocks * rows * count,
    )


def weighted(value, protos):
    return jnp.dot(bare(value), protos, preferred_element_type=jnp.float32)


def row_of(combine, value):
    return combine(value.T, axis=0, keepdims=True)


def pred_logits(preds, protos, raws, top, j):
    raw = scores(preds[...], protos)
    raws[j] = raw
    top[...] = jnp.maximum(top[...], lane_fold(jnp.maximum, raw))


def pred_pull(protos, raws, top, total, pull):
    width = raws.shape[2]
    stats = [row_of(jnp.max, top[...]) * pred_scale]
    peak = jnp.max(top[...], axis=1, keepdims=True)
    top[...] = jnp.broadcast_to(peak, top.shape)
    total[...] = jnp.zeros(total.shape, jnp.float32)
    pull[...] = jnp.zeros(pull.shape, jnp.float32)

    def step(j, protos):
        peak = jnp.concatenate([top[...]] * (width // 128), axis=1)
        value = jnp.exp2((raws[j] - peak) * pred_scale)
        total[...] += lane_fold(jnp.add, value)
        pull[...] += weighted(value, protos)

    over_chunks(protos, width, step)
    return pull[...], [*stats, row_of(jnp.sum, total[...])]


def target_step(codes, protos, stats, other, total, pull, j):
    count = stats.shape[0] // 2
    here, there = stats[j], other[(j + count) % (2 * count)]
    peak = jnp.maximum(here[0:1], there[0:1])
    mass = here[1:2] * jnp.exp2((here[0:1] - peak) * code_scale) + there[1:2] * jnp.exp2(
        (there[0:1] - peak) * code_scale
    )
    offset = peak * code_scale + jnp.log2(mass)
    value = jnp.exp2(scores(codes[...], protos) * code_scale - offset)
    total[...] += lane_fold(jnp.add, value)
    pull[...] += weighted(value, protos)


def target_stats(preds, total, pull):
    cross = lane_fold(jnp.add, pull[...] * preds[...].astype(jnp.float32))
    return [row_of(jnp.sum, total[...]), row_of(jnp.sum, cross)]


def pred_kernel(info, preds, near, across, *refs):
    *outs, raws, top, total, pull, flipped = refs
    protos = near, across
    top[...] = jnp.full(top.shape, low, jnp.float32)
    over_chunks(protos, raws.shape[2], lambda j, part: pred_logits(preds, part, raws, top, j))
    send(info, 0, *pred_pull(protos, raws, top, total, pull), *outs, flipped)


def target_kernel(info, codes, preds, near, across, stats, other, *refs):
    *refs, total, pull, flipped = refs
    earlier, outs = refs[: len(refs) // 2], refs[len(refs) // 2 :]
    total[...] = jnp.zeros(total.shape, jnp.float32)
    pull[...] = jnp.zeros(pull.shape, jnp.float32)
    over_chunks(
        (near, across),
        stats.shape[2],
        lambda j, part: target_step(codes, part, stats, other, total, pull, j),
        True,
    )
    send(info, 0, pull[...], target_stats(preds, total, pull), *outs, flipped)
    for part, out in zip(earlier, outs):
        out[part.shape[0] :, :] = part[...]


def both_kernel(info, *refs):
    *quarters, preds, near, across, stats, other, kept, sent = refs[:-6]
    raws, top, total, pull, flipped, codes = refs[-6:]
    protos = near, across
    placed_rows(info, quarters, codes)
    top[...] = jnp.full(top.shape, low, jnp.float32)
    total[...] = jnp.zeros(total.shape, jnp.float32)
    pull[...] = jnp.zeros(pull.shape, jnp.float32)

    def step(j, part):
        pred_logits(preds, part, raws, top, j)
        target_step(codes, part, stats, other, total, pull, j)

    over_chunks(protos, stats.shape[2], step)
    send(info, 0, pull[...], target_stats(preds, total, pull), kept, sent, flipped)
    send(info, 1, *pred_pull(protos, raws, top, total, pull), kept, sent, flipped)


def rows_part(info, codes, preds, protos, stats, other, rows, proto_count, aways, earlier):
    count, dim = protos[0].shape
    share = dim // proto_count
    width, blocks = min(chunk, count), max(len(aways), 1)
    shapes = [(2 * count // width, rows, width), (rows, 128), (rows, 128), (rows, dim), (dim, rows)]
    scratch = [pltpu.VMEM(shape, jnp.float32) for shape in shapes]
    away = lambda i: aways[0] + i * (aways[1] - aways[0] if len(aways) > 1 else 0)
    if codes is None:
        kernel, ins = pred_kernel, [preds, *protos]
        specs = [whole(value) for value in ins]
    elif not aways:
        kernel, ins = target_kernel, [codes, preds, *protos, stats, other, *earlier]
        specs, scratch = [whole(value) for value in ins], scratch[2:]
    else:
        kernel, ins = both_kernel, [*codes, preds, *protos, stats, other]
        quarter = pl.BlockSpec((1, *codes[0].shape[1:]), lambda i, info: (away(i) - 1, 0, 0))
        block = pl.BlockSpec((rows, dim), lambda i, info: (info[0] ^ away(i), 0))
        specs = [quarter] * len(codes) + [block] + [whole(value) for value in ins[-4:]]
        scratch = [*scratch, pltpu.VMEM((rows, dim), jnp.bfloat16)]
    parts, work = 2 if codes is not None else 1, 2 if aways else 1
    high, tall = parts * (share + stat_rows), parts * (share + sent_rows)
    outs = [jax.ShapeDtypeStruct((high, blocks * rows), jnp.float32)]
    out_specs = [pl.BlockSpec((high, rows), lambda i, info: (0, i))]
    if aways:
        outs.append(jax.ShapeDtypeStruct((proto_count, tall, blocks * rows), jnp.bfloat16))
        out_specs.append(pl.BlockSpec((proto_count, tall, rows), lambda i, info: (0, 0, i)))
    else:
        outs += [jax.ShapeDtypeStruct((tall, rows), jnp.bfloat16)] * (proto_count - 1)
        out_specs += [whole(out) for out in outs[1:]]
    return call(
        kernel, "rows_part", info, (blocks,), ins, specs, outs, out_specs, scratch,
        blocks * work * 8 * rows * count * dim, blocks * work * 2 * rows * count,
    )


def chosen(here, kept, other):
    pull, stats = kept
    far_pull, far_stats = other
    return jnp.where(here, pull, far_pull), [
        jnp.where(here, mine, theirs) for mine, theirs in zip(stats, far_stats)
    ]


names = ["target", "pred"]


def packed_far(target, pred):
    pull, stats = pred
    high = bare(pull)
    rest = bare(pull - high.astype(jnp.float32))
    return jnp.concatenate([bare(target[0]), high, rest, split_stats([*target[1], *stats])], axis=0)


def parted_far(value):
    share = (value.shape[0] - sent_rows) // 3
    target, high, rest = [
        value[i * share : (i + 1) * share, :].astype(jnp.float32) for i in range(3)
    ]
    stats = join_stats(value[3 * share :, :], 4)
    return {"target": (target, stats[:2]), "pred": (high + rest, stats[2:])}


def spread_kernel(info, kept, arrived, *outs):
    high, tall = kept.shape[0] // len(names), arrived.shape[1] // len(names)
    rows = outs[0].shape[1]
    for block, out in enumerate(outs):
        at = slice(block * rows, (block + 1) * rows)
        results = []
        for i, name in enumerate(names):
            mine = parted(kept[i * high : (i + 1) * high, at])
            parts = [
                chosen(info[1] == s, mine, parted_sent(arrived[s, i * tall : (i + 1) * tall, at]))
                for s in range(arrived.shape[0])
            ]
            results.append(joins[name](parts))
        out[...] = packed_far(*results)


def join_spread(info, kept, arrived, rows):
    share = kept.shape[0] // len(names) - stat_rows
    outs = [
        jax.ShapeDtypeStruct((3 * share + sent_rows, rows), jnp.bfloat16)
        for _ in range(kept.shape[1] // rows)
    ]
    return call(
        spread_kernel, "join_spread", info, (1,), [kept, arrived], [whole(kept), whole(arrived)],
        outs, [whole(out) for out in outs], [], 1 << 20, 0,
    )


def final_kernel(count, info, *refs):
    kept, sent, (loss, pull) = refs[0], refs[1:count], refs[-2:]
    far = [parted_far(part[...]) for part in refs[count:-2]]
    high, tall = kept.shape[0] // len(names), sent[0].shape[0] // len(names)
    target, pred = [
        joins[name](
            [parted(kept[i * high : (i + 1) * high, :])]
            + [parted_sent(part[i * tall : (i + 1) * tall, :]) for part in sent]
            + [part[name] for part in far]
        )
        for i, name in enumerate(names)
    ]
    (target, (mass, cross)), (pred, (peak, total)) = target, pred
    pull[...] = target / mass - pred / total
    loss[...] = peak * log2 + jnp.log(total) - cross / mass / pred_temp


def finish(info, own, others):
    high, length = own[0].shape
    outs = [
        jax.ShapeDtypeStruct((1, length), jnp.float32),
        jax.ShapeDtypeStruct((high // len(names) - stat_rows, length), jnp.float32),
    ]
    ins = [*own, *others]
    return call(
        functools.partial(final_kernel, len(own)), "finish", info, (1,), ins,
        [whole(value) for value in ins], outs, [whole(out) for out in outs], [], 1 << 20, 0,
    )[1:]


def swap(value, axis, bits):
    count = lax.axis_size(axis)
    return lax.ppermute(value, axis, [(i, i ^ bits) for i in range(count)])


def body(codes_view, pred_view, prototypes):
    rows = codes_view.shape[0]
    dp_count, proto_count = lax.axis_size("dp"), lax.axis_size("proto")
    z_count = dp_count // 2
    me, proto = lax.axis_index("dp"), lax.axis_index("proto")
    info = jnp.stack([me // 2, proto]).astype(jnp.int32)
    same_core = [[2 * z + core for z in range(z_count)] for core in range(2)]

    def rows_of(info, codes, preds, aways, earlier):
        return rows_part(
            info, codes, preds, protos, stats, other, rows, proto_count, aways, earlier
        )

    def far_rows(info, aways):
        info, kept, out = rows_of(info, codes, preds, aways, None)
        return info, kept, lax.all_to_all(out, "proto", 0, 0)

    protos = prototypes, swap(prototypes, "dp", 1)
    part = rows // proto_count
    piece = lax.dynamic_slice_in_dim(codes_view, proto * part, part, 0)
    quarters = [swap(piece, "dp", 2 * t) for t in range(1, z_count)]
    preds = lax.all_gather(pred_view, "dp", axis=0, tiled=True, axis_index_groups=same_core)

    stats = other = None
    info, stats = stats_part(info, [codes_view], protos, None, rows)
    quarters, info = lax.optimization_barrier((quarters, info))
    quarters = jnp.stack(quarters)
    codes = [quarters] + [swap(quarters, "proto", s) for s in range(1, proto_count)]
    info, *earlier = rows_of(info, None, pred_view, (), None)
    info, stats = stats_part(info, codes, protos, stats, rows)
    other = swap(stats, "dp", 1)

    aways = range(z_count - 1, 1, -1)
    info, far_kept, far_arrived = far_rows(info, aways)
    info, next_kept, next_arrived = far_rows(info, (1,))
    info, *far = join_spread(info, far_kept, far_arrived, rows)
    far = [swap(part, "dp", 2 * away) for away, part in zip(aways, far)]
    info, kept, *out = rows_of(info, codes_view, pred_view, (), earlier)
    own = [kept] + [swap(value, "proto", s) for s, value in enumerate(out, 1)]
    far[:1], next_arrived = lax.optimization_barrier((far[:1], next_arrived))
    info, part = join_spread(info, next_kept, next_arrived, rows)
    loss, pull = finish(info, own, [*far, swap(part, "dp", 2)])
    return (loss.reshape(rows), pull.T)


def solution(mesh):
    placed = (P("dp", None), P("dp", None), P(("proto", "dp"), None))
    return jax.shard_map(
        body, mesh=mesh, in_specs=placed, out_specs=(P("dp"), P("dp", "proto")), check_vma=False
    )
```

```python
import functools
import math

import jax
import jax.numpy as jnp
from jax import lax
from jax.experimental import pallas as pl
from jax.experimental.pallas import tpu as pltpu
from jax.sharding import PartitionSpec as P

code_temp = 0.05
pred_temp = 0.1
code_scale = math.log2(math.e) / code_temp
pred_scale = math.log2(math.e) / pred_temp
log2 = math.log(2.0)
stat_rows = 8
sent_rows = 16
low = -1e30
chunk = 512
mebi = 1024 * 1024


def scores(embeds, protos):
    return lax.dot_general(
        embeds, protos, (((1,), (1,)), ((), ())), preferred_element_type=jnp.float32
    )


def bare(value):
    return value.astype(jnp.bfloat16)


def add(parts):
    return functools.reduce(jnp.add, parts)


def lane_fold(combine, value):
    parts = [value[:, i : i + 128] for i in range(0, value.shape[1], 128)]
    return functools.reduce(combine, parts)


def padded(rows, width):
    filler = jnp.zeros((stat_rows - len(rows), width), jnp.float32)
    return jnp.concatenate([*rows, filler], axis=0)


def split_stats(stats):
    terms = []
    for row in stats:
        for _ in range(3):
            term = bare(row)
            row = row - term.astype(jnp.float32)
            terms.append(term)
    filler = jnp.zeros((sent_rows - len(terms), stats[0].shape[1]), jnp.bfloat16)
    return jnp.concatenate([*terms, filler], axis=0)


def join_stats(terms, count):
    wide = terms.astype(jnp.float32)
    return [add([wide[3 * i + j : 3 * i + j + 1] for j in range(3)]) for i in range(count)]


def parted(value):
    share = value.shape[0] - stat_rows
    return value[:share, :], [value[share + i : share + i + 1, :] for i in range(2)]


def parted_sent(value):
    share = value.shape[0] - sent_rows
    return value[:share, :].astype(jnp.float32), join_stats(value[share:, :], 2)


def packed(part):
    pull, stats = part
    return jnp.concatenate([pull, padded(stats, pull.shape[1])], axis=0)


def join_preds(parts):
    peak = functools.reduce(jnp.maximum, [stats[0] for _, stats in parts])
    factors = [jnp.exp2(stats[0] - peak) for _, stats in parts]
    pull = add([part * factor for (part, _), factor in zip(parts, factors)])
    total = add([stats[1] * factor for (_, stats), factor in zip(parts, factors)])
    return pull, [peak, total]


def join_targets(parts):
    stats = [add([stats[i] for _, stats in parts]) for i in range(2)]
    return add([part for part, _ in parts]), stats


joins = {"pred": join_preds, "target": join_targets}


def send(info, place, pull, stats, kept, *sent):
    *sent, flipped = sent
    whole = len(sent) == 1
    count = sent[0].shape[0] if whole else len(sent) + 1
    share = pull.shape[1] // count
    high, tall = share + stat_rows, share + sent_rows
    flipped[...] = pull.T
    mine = pl.multiple_of(info[1] * share, share)
    kept[place * high : place * high + share, :] = flipped[pl.ds(mine, share), :]
    kept[place * high + share : (place + 1) * high, :] = padded(stats, pull.shape[0])
    terms = split_stats(stats)
    for s in range(count) if whole else range(1, count):
        out, start = sent[0].at[s] if whole else sent[s - 1], s * share
        if not whole:
            start = pl.multiple_of((info[1] ^ s) * share, share)
        out[place * tall : place * tall + share, :] = bare(flipped[pl.ds(start, share), :])
        out[place * tall + share : (place + 1) * tall, :] = terms


def whole(value):
    return pl.BlockSpec(value.shape, lambda *_: (0,) * len(value.shape))


def call(kernel, name, info, grid, ins, in_specs, outs, out_specs, scratch, flops, exps, room):
    values = pl.pallas_call(
        kernel,
        grid_spec=pltpu.PrefetchScalarGridSpec(
            num_scalar_prefetch=1,
            grid=grid,
            in_specs=in_specs,
            out_specs=out_specs,
            scratch_shapes=scratch,
        ),
        out_shape=outs,
        compiler_params=pltpu.CompilerParams(vmem_limit_bytes=room * mebi),
        cost_estimate=pl.CostEstimate(flops=flops, bytes_accessed=flops // 128, transcendentals=exps),
        name=name,
    )(info, *ins)
    info, first = lax.optimization_barrier((info, values[0]))
    return info, first, *values[1:]


def placed_rows(info, quarters, block):
    part = quarters[0].shape[1]
    for s, quarter in enumerate(quarters):
        place = pl.multiple_of((info[1] ^ s) * part, part)
        block[pl.ds(place, part), :] = quarter[0]


def over_chunks(protos, width, step, unrolled=False):
    count = protos[0].shape[0] // width
    if unrolled:
        for i in range(count):
            for half, part in enumerate(protos):
                step(half * count + i, part[i * width : (i + 1) * width, :])
        return

    def both(i, carry):
        at = pl.ds(pl.multiple_of(i * width, width), width)
        for half, part in enumerate(protos):
            step(half * count + i, part[at, :])
        return carry

    lax.fori_loop(0, count, both, 0)


def stats_kernel(fresh, info, *refs):
    if fresh:
        block, *protos, stats = refs
    else:
        *codes, near, across, before, stats, block = refs
        protos = near, across
        placed_rows(info, codes, block)

    @pl.when(pl.program_id(0) == 0)
    def _():
        if fresh:
            stats[:, 0:1, :] = jnp.full((stats.shape[0], 1, stats.shape[2]), low, jnp.float32)
            stats[:, 1:, :] = jnp.zeros((stats.shape[0], stat_rows - 1, stats.shape[2]), jnp.float32)
        else:
            stats[...] = before[...]

    def step(j, protos):
        raw = scores(block[...], protos)
        old, total = stats[j, 0:1, :], stats[j, 1:2, :]
        new = jnp.maximum(old, jnp.max(raw, axis=0, keepdims=True))
        value = jnp.exp2((raw - new) * code_scale)
        stats[j, 1:2, :] = total * jnp.exp2((old - new) * code_scale) + jnp.sum(
            value, axis=0, keepdims=True
        )
        stats[j, 0:1, :] = new

    over_chunks(protos, stats.shape[2], step, True)


def stats_part(info, codes, protos, before, rows):
    count, dim = protos[0].shape
    width = min(chunk, count)
    fresh = before is None
    ins = [*codes, *protos]
    if fresh:
        blocks, scratch = 1, []
        specs = [whole(value) for value in ins]
    else:
        blocks, scratch = codes[0].shape[0], [pltpu.VMEM((rows, dim), jnp.bfloat16)]
        ins = [*ins, before]
        specs = [pl.BlockSpec((1, *part.shape[1:]), lambda i, info: (i, 0, 0)) for part in codes]
        specs += [whole(value) for value in ins[-3:]]
    out = jax.ShapeDtypeStruct((2 * count // width, stat_rows, width), jnp.float32)
    return call(
        functools.partial(stats_kernel, fresh), "stats_part", info, (blocks,), ins, specs, [out],
        [whole(out)], scratch, 4 * blocks * rows * count * dim, 2 * blocks * rows * count, 6,
    )


def weighted(value, protos):
    return jnp.dot(bare(value), protos, preferred_element_type=jnp.float32)


def row_of(combine, value):
    return combine(value.T, axis=0, keepdims=True)


def pred_logits(preds, protos, raws, top, j):
    raw = scores(preds[...], protos)
    raws[j] = raw
    top[...] = jnp.maximum(top[...], lane_fold(jnp.maximum, raw))


def pred_pull(protos, raws, top, total, pull):
    width = raws.shape[2]
    stats = [row_of(jnp.max, top[...]) * pred_scale]
    peak = jnp.max(top[...], axis=1, keepdims=True)
    top[...] = jnp.broadcast_to(peak, top.shape)
    total[...] = jnp.zeros(total.shape, jnp.float32)
    pull[...] = jnp.zeros(pull.shape, jnp.float32)

    def step(j, protos):
        peak = jnp.concatenate([top[...]] * (width // 128), axis=1)
        value = jnp.exp2((raws[j] - peak) * pred_scale)
        total[...] += lane_fold(jnp.add, value)
        pull[...] += weighted(value, protos)

    over_chunks(protos, width, step)
    return pull[...], [*stats, row_of(jnp.sum, total[...])]


def target_step(codes, protos, stats, other, total, pull, j):
    count = stats.shape[0] // 2
    here, there = stats[j], other[(j + count) % (2 * count)]
    peak = jnp.maximum(here[0:1], there[0:1])
    mass = here[1:2] * jnp.exp2((here[0:1] - peak) * code_scale) + there[1:2] * jnp.exp2(
        (there[0:1] - peak) * code_scale
    )
    offset = peak * code_scale + jnp.log2(mass)
    value = jnp.exp2(scores(codes[...], protos) * code_scale - offset)
    total[...] += lane_fold(jnp.add, value)
    pull[...] += weighted(value, protos)


def target_stats(preds, total, pull):
    cross = lane_fold(jnp.add, pull[...] * preds[...].astype(jnp.float32))
    return [row_of(jnp.sum, total[...]), row_of(jnp.sum, cross)]


def pred_kernel(info, preds, near, across, *refs):
    *outs, raws, top, total, pull, flipped = refs
    protos = near, across
    top[...] = jnp.full(top.shape, low, jnp.float32)
    over_chunks(protos, raws.shape[2], lambda j, part: pred_logits(preds, part, raws, top, j))
    send(info, 0, *pred_pull(protos, raws, top, total, pull), *outs, flipped)


def target_kernel(info, codes, preds, near, across, stats, other, *refs):
    *refs, total, pull, flipped = refs
    earlier, outs = refs[: len(refs) // 2], refs[len(refs) // 2 :]
    total[...] = jnp.zeros(total.shape, jnp.float32)
    pull[...] = jnp.zeros(pull.shape, jnp.float32)
    over_chunks(
        (near, across),
        stats.shape[2],
        lambda j, part: target_step(codes, part, stats, other, total, pull, j),
        True,
    )
    send(info, 0, pull[...], target_stats(preds, total, pull), *outs, flipped)
    for part, out in zip(earlier, outs):
        out[part.shape[0] :, :] = part[...]


def both_kernel(info, *refs):
    *quarters, preds, near, across, stats, other, kept, sent = refs[:-6]
    raws, top, total, pull, flipped, codes = refs[-6:]
    protos = near, across
    placed_rows(info, quarters, codes)
    top[...] = jnp.full(top.shape, low, jnp.float32)
    total[...] = jnp.zeros(total.shape, jnp.float32)
    pull[...] = jnp.zeros(pull.shape, jnp.float32)

    def step(j, part):
        pred_logits(preds, part, raws, top, j)
        target_step(codes, part, stats, other, total, pull, j)

    over_chunks(protos, stats.shape[2], step)
    send(info, 0, pull[...], target_stats(preds, total, pull), kept, sent, flipped)
    send(info, 1, *pred_pull(protos, raws, top, total, pull), kept, sent, flipped)


def rows_part(info, codes, preds, protos, stats, other, rows, proto_count, aways, earlier):
    count, dim = protos[0].shape
    share = dim // proto_count
    width, blocks = min(chunk, count), max(len(aways), 1)
    shapes = [(2 * count // width, rows, width), (rows, 128), (rows, 128), (rows, dim), (dim, rows)]
    scratch = [pltpu.VMEM(shape, jnp.float32) for shape in shapes]
    away = lambda i: aways[0] + i * (aways[1] - aways[0] if len(aways) > 1 else 0)
    if codes is None:
        kernel, ins = pred_kernel, [preds, *protos]
        specs = [whole(value) for value in ins]
    elif not aways:
        kernel, ins = target_kernel, [codes, preds, *protos, stats, other, *earlier]
        specs, scratch = [whole(value) for value in ins], scratch[2:]
    else:
        kernel, ins = both_kernel, [*codes, preds, *protos, stats, other]
        quarter = pl.BlockSpec((1, *codes[0].shape[1:]), lambda i, info: (away(i) - 1, 0, 0))
        block = pl.BlockSpec((rows, dim), lambda i, info: (info[0] ^ away(i), 0))
        specs = [quarter] * len(codes) + [block] + [whole(value) for value in ins[-4:]]
        scratch = [*scratch, pltpu.VMEM((rows, dim), jnp.bfloat16)]
    parts, work = 2 if codes is not None else 1, 2 if aways else 1
    high, tall = parts * (share + stat_rows), parts * (share + sent_rows)
    outs = [jax.ShapeDtypeStruct((high, blocks * rows), jnp.float32)]
    out_specs = [pl.BlockSpec((high, rows), lambda i, info: (0, i))]
    if aways:
        outs.append(jax.ShapeDtypeStruct((proto_count, tall, blocks * rows), jnp.bfloat16))
        out_specs.append(pl.BlockSpec((proto_count, tall, rows), lambda i, info: (0, 0, i)))
    else:
        outs += [jax.ShapeDtypeStruct((tall, rows), jnp.bfloat16)] * (proto_count - 1)
        out_specs += [whole(out) for out in outs[1:]]
    return call(
        kernel, "rows_part", info, (blocks,), ins, specs, outs, out_specs, scratch,
        blocks * work * 8 * rows * count * dim, blocks * work * 2 * rows * count,
        6 if kernel is target_kernel else 14,
    )


def chosen(here, kept, other):
    pull, stats = kept
    far_pull, far_stats = other
    return jnp.where(here, pull, far_pull), [
        jnp.where(here, mine, theirs) for mine, theirs in zip(stats, far_stats)
    ]


names = ["target", "pred"]


def packed_far(target, pred):
    pull, stats = pred
    high = bare(pull)
    rest = bare(pull - high.astype(jnp.float32))
    return jnp.concatenate([bare(target[0]), high, rest, split_stats([*target[1], *stats])], axis=0)


def parted_far(value):
    share = (value.shape[0] - sent_rows) // 3
    target, high, rest = [
        value[i * share : (i + 1) * share, :].astype(jnp.float32) for i in range(3)
    ]
    stats = join_stats(value[3 * share :, :], 4)
    return {"target": (target, stats[:2]), "pred": (high + rest, stats[2:])}


def spread_kernel(info, kept, arrived, *outs):
    high, tall = kept.shape[0] // len(names), arrived.shape[1] // len(names)
    rows = outs[0].shape[1]
    for block, out in enumerate(outs):
        at = slice(block * rows, (block + 1) * rows)
        results = []
        for i, name in enumerate(names):
            mine = parted(kept[i * high : (i + 1) * high, at])
            parts = [
                chosen(info[1] == s, mine, parted_sent(arrived[s, i * tall : (i + 1) * tall, at]))
                for s in range(arrived.shape[0])
            ]
            results.append(joins[name](parts))
        out[...] = packed_far(*results)


def join_spread(info, kept, arrived, rows):
    share = kept.shape[0] // len(names) - stat_rows
    outs = [
        jax.ShapeDtypeStruct((3 * share + sent_rows, rows), jnp.bfloat16)
        for _ in range(kept.shape[1] // rows)
    ]
    return call(
        spread_kernel, "join_spread", info, (1,), [kept, arrived], [whole(kept), whole(arrived)],
        outs, [whole(out) for out in outs], [], 1 << 20, 0, 5,
    )


def final_kernel(count, info, *refs):
    kept, sent, (loss, pull) = refs[0], refs[1:count], refs[-2:]
    far = [parted_far(part[...]) for part in refs[count:-2]]
    high, tall = kept.shape[0] // len(names), sent[0].shape[0] // len(names)
    target, pred = [
        joins[name](
            [parted(kept[i * high : (i + 1) * high, :])]
            + [parted_sent(part[i * tall : (i + 1) * tall, :]) for part in sent]
            + [part[name] for part in far]
        )
        for i, name in enumerate(names)
    ]
    (target, (mass, cross)), (pred, (peak, total)) = target, pred
    pull[...] = target / mass - pred / total
    loss[...] = peak * log2 + jnp.log(total) - cross / mass / pred_temp


def finish(info, own, others):
    high, length = own[0].shape
    outs = [
        jax.ShapeDtypeStruct((1, length), jnp.float32),
        jax.ShapeDtypeStruct((high // len(names) - stat_rows, length), jnp.float32),
    ]
    ins = [*own, *others]
    return call(
        functools.partial(final_kernel, len(own)), "finish", info, (1,), ins,
        [whole(value) for value in ins], outs, [whole(out) for out in outs], [], 1 << 20, 0, 5,
    )[1:]


def swap(value, axis, bits):
    count = lax.axis_size(axis)
    return lax.ppermute(value, axis, [(i, i ^ bits) for i in range(count)])


def body(codes_view, pred_view, prototypes):
    rows = codes_view.shape[0]
    dp_count, proto_count = lax.axis_size("dp"), lax.axis_size("proto")
    z_count = dp_count // 2
    me, proto = lax.axis_index("dp"), lax.axis_index("proto")
    info = jnp.stack([me // 2, proto]).astype(jnp.int32)
    same_core = [[2 * z + core for z in range(z_count)] for core in range(2)]

    def rows_of(info, codes, preds, aways, earlier):
        return rows_part(
            info, codes, preds, protos, stats, other, rows, proto_count, aways, earlier
        )

    def far_rows(info, aways):
        info, kept, out = rows_of(info, codes, preds, aways, None)
        return info, kept, lax.all_to_all(out, "proto", 0, 0)

    protos = prototypes, swap(prototypes, "dp", 1)
    part = rows // proto_count
    piece = lax.dynamic_slice_in_dim(codes_view, proto * part, part, 0)
    quarters = [swap(piece, "dp", 2 * t) for t in range(1, z_count)]
    preds = lax.all_gather(pred_view, "dp", axis=0, tiled=True, axis_index_groups=same_core)

    stats = other = None
    info, stats = stats_part(info, [codes_view], protos, None, rows)
    quarters, info = lax.optimization_barrier((quarters, info))
    quarters = jnp.stack(quarters)
    codes = [quarters] + [swap(quarters, "proto", s) for s in range(1, proto_count)]
    info, *earlier = rows_of(info, None, pred_view, (), None)
    info, stats = stats_part(info, codes, protos, stats, rows)
    other = swap(stats, "dp", 1)

    aways = range(z_count - 1, 1, -1)
    info, far_kept, far_arrived = far_rows(info, aways)
    info, next_kept, next_arrived = far_rows(info, (1,))
    info, *far = join_spread(info, far_kept, far_arrived, rows)
    far = [swap(part, "dp", 2 * away) for away, part in zip(aways, far)]
    info, kept, *out = rows_of(info, codes_view, pred_view, (), earlier)
    own = [kept] + [swap(value, "proto", s) for s, value in enumerate(out, 1)]
    far[:1], next_arrived = lax.optimization_barrier((far[:1], next_arrived))
    info, part = join_spread(info, next_kept, next_arrived, rows)
    own, part = lax.optimization_barrier((own, part))
    loss, pull = finish(info, own, [*far, swap(part, "dp", 2)])
    return (loss.reshape(rows), pull.T)


def solution(mesh):
    placed = (P("dp", None), P("dp", None), P(("proto", "dp"), None))
    return jax.shard_map(
        body, mesh=mesh, in_specs=placed, out_specs=(P("dp"), P("dp", "proto")), check_vma=False
    )
```

```python
import functools
import math

import jax
import jax.numpy as jnp
from jax import lax
from jax.experimental import pallas as pl
from jax.experimental.pallas import tpu as pltpu
from jax.sharding import PartitionSpec as P

code_temp = 0.05
pred_temp = 0.1
code_scale = math.log2(math.e) / code_temp
pred_scale = math.log2(math.e) / pred_temp
log2 = math.log(2.0)
stat_rows = 8
sent_rows = 16
low = -1e30
chunk = 512
mebi = 1024 * 1024


def scores(embeds, protos):
    return lax.dot_general(
        embeds, protos, (((1,), (1,)), ((), ())), preferred_element_type=jnp.float32
    )


def bare(value):
    return value.astype(jnp.bfloat16)


def add(parts):
    return functools.reduce(jnp.add, parts)


def lane_fold(combine, value):
    parts = [value[:, i : i + 128] for i in range(0, value.shape[1], 128)]
    return functools.reduce(combine, parts)


def padded(rows, width):
    filler = jnp.zeros((stat_rows - len(rows), width), jnp.float32)
    return jnp.concatenate([*rows, filler], axis=0)


def split_stats(stats):
    terms = []
    for row in stats:
        for _ in range(3):
            term = bare(row)
            row = row - term.astype(jnp.float32)
            terms.append(term)
    filler = jnp.zeros((sent_rows - len(terms), stats[0].shape[1]), jnp.bfloat16)
    return jnp.concatenate([*terms, filler], axis=0)


def join_stats(terms, count):
    wide = terms.astype(jnp.float32)
    return [add([wide[3 * i + j : 3 * i + j + 1] for j in range(3)]) for i in range(count)]


def parted(value):
    share = value.shape[0] - stat_rows
    return value[:share, :], [value[share + i : share + i + 1, :] for i in range(2)]


def parted_sent(value):
    share = value.shape[0] - sent_rows
    return value[:share, :].astype(jnp.float32), join_stats(value[share:, :], 2)


def packed(part):
    pull, stats = part
    return jnp.concatenate([pull, padded(stats, pull.shape[1])], axis=0)


def join_preds(parts):
    peak = functools.reduce(jnp.maximum, [stats[0] for _, stats in parts])
    factors = [jnp.exp2(stats[0] - peak) for _, stats in parts]
    pull = add([part * factor for (part, _), factor in zip(parts, factors)])
    total = add([stats[1] * factor for (_, stats), factor in zip(parts, factors)])
    return pull, [peak, total]


def join_targets(parts):
    stats = [add([stats[i] for _, stats in parts]) for i in range(2)]
    return add([part for part, _ in parts]), stats


joins = {"pred": join_preds, "target": join_targets}


def send(info, place, pull, stats, outs, flipped):
    kept, *sent = outs
    share = pull.shape[1] // len(outs)
    high, tall = share + stat_rows, share + sent_rows
    flipped[...] = pull.T
    mine = pl.multiple_of(info[1] * share, share)
    kept[place * high : place * high + share, :] = flipped[pl.ds(mine, share), :]
    kept[place * high + share : (place + 1) * high, :] = padded(stats, pull.shape[0])
    terms = split_stats(stats)
    for s, out in enumerate(sent, 1):
        start = pl.multiple_of((info[1] ^ s) * share, share)
        out[place * tall : place * tall + share, :] = bare(flipped[pl.ds(start, share), :])
        out[place * tall + share : (place + 1) * tall, :] = terms


def whole(value):
    return pl.BlockSpec(value.shape, lambda *_: (0,) * len(value.shape))


def call(kernel, name, info, grid, ins, in_specs, outs, out_specs, scratch, flops, exps, room, passed=()):
    count, total = len(ins), len(ins) + len(outs)

    def without(*refs):
        return kernel(*refs[: 1 + total], *refs[1 + total + len(passed) :])

    outs = [*outs, *[jax.ShapeDtypeStruct(ins[i].shape, ins[i].dtype) for i in passed]]
    out_specs = [*out_specs, *[pl.BlockSpec(memory_space=pl.ANY)] * len(passed)]
    values = pl.pallas_call(
        without,
        grid_spec=pltpu.PrefetchScalarGridSpec(
            num_scalar_prefetch=1,
            grid=grid,
            in_specs=in_specs,
            out_specs=out_specs,
            scratch_shapes=scratch,
        ),
        out_shape=outs,
        input_output_aliases={1 + i: total - count + k for k, i in enumerate(passed)},
        compiler_params=pltpu.CompilerParams(vmem_limit_bytes=room * mebi),
        cost_estimate=pl.CostEstimate(flops=flops, bytes_accessed=flops // 128, transcendentals=exps),
        name=name,
    )(info, *ins)
    info, first = lax.optimization_barrier((info, values[0]))
    return info, first, *values[1:]


def placed_rows(info, quarters, block):
    part = quarters[0].shape[1]
    for s, quarter in enumerate(quarters):
        place = pl.multiple_of((info[1] ^ s) * part, part)
        block[pl.ds(place, part), :] = quarter[0]


def over_chunks(protos, width, step, unrolled=False):
    count = protos[0].shape[0] // width
    if unrolled:
        for i in range(count):
            for half, part in enumerate(protos):
                step(half * count + i, part[i * width : (i + 1) * width, :])
        return

    def both(i, carry):
        at = pl.ds(pl.multiple_of(i * width, width), width)
        for half, part in enumerate(protos):
            step(half * count + i, part[at, :])
        return carry

    lax.fori_loop(0, count, both, 0)


def stats_kernel(fresh, info, *refs):
    if fresh:
        *codes, near, across, stats, copied = refs
        copied[...] = near[...]
        stats[:, 0:1, :] = jnp.full((stats.shape[0], 1, stats.shape[2]), low, jnp.float32)
        stats[:, 1:, :] = jnp.zeros((stats.shape[0], stat_rows - 1, stats.shape[2]), jnp.float32)
    else:
        *codes, near, across, before, stats = refs
        stats[...] = before[...]
    for part in codes:
        rows = part[...].reshape(-1, part.shape[-1])

        def step(j, protos):
            raw = scores(rows, protos)
            old, total = stats[j, 0:1, :], stats[j, 1:2, :]
            new = jnp.maximum(old, jnp.max(raw, axis=0, keepdims=True))
            value = jnp.exp2((raw - new) * code_scale)
            stats[j, 1:2, :] = total * jnp.exp2((old - new) * code_scale) + jnp.sum(
                value, axis=0, keepdims=True
            )
            stats[j, 0:1, :] = new

        over_chunks((near, across), stats.shape[2], step, True)


def stats_part(info, codes, protos, before):
    count, dim = protos[0].shape
    width = min(chunk, count)
    rows = sum(math.prod(part.shape[:-1]) for part in codes)
    outs = [jax.ShapeDtypeStruct((2 * count // width, stat_rows, width), jnp.float32)]
    ins, passed = [*codes, *protos], [len(codes), len(codes) + 1]
    if before is None:
        outs.append(jax.ShapeDtypeStruct(protos[0].shape, protos[0].dtype))
        passed = passed[1:]
    else:
        ins.append(before)
    return call(
        functools.partial(stats_kernel, before is None), "stats_part", info, (1,), ins,
        [whole(value) for value in ins], outs, [whole(out) for out in outs], [],
        4 * rows * count * dim, 2 * rows * count, 6, passed,
    )


def offset_kernel(info, stats, other, out):
    count = stats.shape[0] // 2
    for j in range(2 * count):
        here, there = stats[j], other[(j + count) % (2 * count)]
        peak = jnp.maximum(here[0:1], there[0:1])
        mass = here[1:2] * jnp.exp2((here[0:1] - peak) * code_scale) + there[1:2] * jnp.exp2(
            (there[0:1] - peak) * code_scale
        )
        offset = peak * code_scale + jnp.log2(mass)
        out[j] = jnp.broadcast_to(offset, out.shape[1:])


def offset_part(info, stats, other):
    return call(
        offset_kernel, "offset_part", info, (1,), [stats, other], [whole(stats)] * 2, [stats],
        [whole(stats)], [], 1 << 20, 0, 5,
    )


def weighted(value, protos):
    return jnp.dot(bare(value), protos, preferred_element_type=jnp.float32)


def row_of(combine, value):
    return combine(value.T, axis=0, keepdims=True)


def pred_logits(preds, protos, raws, top, j):
    raw = scores(preds[...], protos)
    raws[j] = raw
    top[...] = jnp.maximum(top[...], lane_fold(jnp.maximum, raw))


def pred_pull(protos, raws, top, total, pull):
    width = raws.shape[2]
    stats = [row_of(jnp.max, top[...]) * pred_scale]
    peak = jnp.max(top[...], axis=1, keepdims=True)
    top[...] = jnp.broadcast_to(peak, top.shape)
    total[...] = jnp.zeros(total.shape, jnp.float32)
    pull[...] = jnp.zeros(pull.shape, jnp.float32)

    def step(j, protos):
        peak = jnp.concatenate([top[...]] * (width // 128), axis=1)
        value = jnp.exp2((raws[j] - peak) * pred_scale)
        total[...] += lane_fold(jnp.add, value)
        pull[...] += weighted(value, protos)

    over_chunks(protos, width, step)
    return pull[...], [*stats, row_of(jnp.sum, total[...])]


def target_step(codes, protos, offset, total, pull, j):
    value = jnp.exp2(scores(codes[...], protos) * code_scale - offset[j, 0:1, :])
    total[...] += lane_fold(jnp.add, value)
    pull[...] += weighted(value, protos)


def target_stats(preds, total, pull):
    cross = lane_fold(jnp.add, pull[...] * preds[...].astype(jnp.float32))
    return [row_of(jnp.sum, total[...]), row_of(jnp.sum, cross)]


def pred_kernel(info, preds, near, across, *refs):
    *outs, raws, top, total, pull, flipped = refs
    protos = near, across
    top[...] = jnp.full(top.shape, low, jnp.float32)
    over_chunks(protos, raws.shape[2], lambda j, part: pred_logits(preds, part, raws, top, j))
    send(info, 0, *pred_pull(protos, raws, top, total, pull), outs, flipped)


def target_kernel(info, codes, preds, near, across, offset, *refs):
    *refs, total, pull, flipped = refs
    earlier, outs = refs[: len(refs) // 2], refs[len(refs) // 2 :]
    total[...] = jnp.zeros(total.shape, jnp.float32)
    pull[...] = jnp.zeros(pull.shape, jnp.float32)
    over_chunks(
        (near, across),
        offset.shape[2],
        lambda j, part: target_step(codes, part, offset, total, pull, j),
        True,
    )
    send(info, 0, pull[...], target_stats(preds, total, pull), outs, flipped)
    for part, out in zip(earlier, outs):
        out[part.shape[0] :, :] = part[...]


def both_kernel(proto_count, info, *refs):
    *quarters, preds, near, across, offset = refs[: proto_count + 4]
    outs = refs[proto_count + 4 : -6]
    raws, top, total, pull, flipped, codes = refs[-6:]
    protos = near, across
    placed_rows(info, quarters, codes)
    top[...] = jnp.full(top.shape, low, jnp.float32)
    total[...] = jnp.zeros(total.shape, jnp.float32)
    pull[...] = jnp.zeros(pull.shape, jnp.float32)

    def step(j, part):
        pred_logits(preds, part, raws, top, j)
        target_step(codes, part, offset, total, pull, j)

    over_chunks(protos, offset.shape[2], step)
    send(info, 0, pull[...], target_stats(preds, total, pull), outs, flipped)
    send(info, 1, *pred_pull(protos, raws, top, total, pull), outs, flipped)


def rows_part(info, codes, preds, protos, offset, rows, proto_count, away, earlier):
    count, dim = protos[0].shape
    share = dim // proto_count
    width = min(chunk, count)
    shapes = [(2 * count // width, rows, width), (rows, 128), (rows, 128), (rows, dim), (dim, rows)]
    scratch = [pltpu.VMEM(shape, jnp.float32) for shape in shapes]
    if codes is None:
        kernel, ins, passed = pred_kernel, [preds, *protos], (1, 2)
        specs = [whole(value) for value in ins]
    elif not away:
        kernel, ins, passed = target_kernel, [codes, preds, *protos, offset, *earlier], ()
        specs, scratch = [whole(value) for value in ins], scratch[2:]
    else:
        kernel, ins = functools.partial(both_kernel, proto_count), [*codes, preds, *protos, offset]
        passed = tuple(len(codes) + i for i in range(3))
        quarter = pl.BlockSpec((1, *codes[0].shape[1:]), lambda i, info: (away - 1, 0, 0))
        block = pl.BlockSpec((rows, dim), lambda i, info: (info[0] ^ away, 0))
        specs = [quarter] * len(codes) + [block] + [whole(value) for value in ins[-3:]]
        scratch = [*scratch, pltpu.VMEM((rows, dim), jnp.bfloat16)]
    parts, work = 2 if codes is not None else 1, 2 if away else 1
    high, tall = parts * (share + stat_rows), parts * (share + sent_rows)
    outs = [jax.ShapeDtypeStruct((high, rows), jnp.float32)]
    outs += [jax.ShapeDtypeStruct((tall, rows), jnp.bfloat16)] * (proto_count - 1)
    return call(
        kernel, "rows_part", info, (1,), ins, specs, outs, [whole(out) for out in outs], scratch,
        work * 8 * rows * count * dim, work * 2 * rows * count,
        6 if kernel is target_kernel else 14, passed,
    )


names = ["target", "pred"]


def packed_far(target, pred):
    pull, stats = pred
    high = bare(pull)
    rest = bare(pull - high.astype(jnp.float32))
    return jnp.concatenate([bare(target[0]), high, rest, split_stats([*target[1], *stats])], axis=0)


def parted_far(value):
    share = (value.shape[0] - sent_rows) // 3
    target, high, rest = [
        value[i * share : (i + 1) * share, :].astype(jnp.float32) for i in range(3)
    ]
    stats = join_stats(value[3 * share :, :], 4)
    return {"target": (target, stats[:2]), "pred": (high + rest, stats[2:])}


def joined(parts, others=()):
    kept, *sent = parts
    high, tall = kept.shape[0] // len(names), sent[0].shape[0] // len(names)
    return [
        joins[name](
            [parted(kept[i * high : (i + 1) * high, :])]
            + [parted_sent(part[i * tall : (i + 1) * tall, :]) for part in sent]
            + [part[name] for part in others]
        )
        for i, name in enumerate(names)
    ]


def spread_kernel(info, *refs):
    *parts, out = refs
    out[...] = packed_far(*joined(parts))


def join_spread(info, parts):
    high, rows = parts[0].shape
    share = high // len(names) - stat_rows
    out = jax.ShapeDtypeStruct((3 * share + sent_rows, rows), jnp.bfloat16)
    return call(
        spread_kernel, "join_spread", info, (1,), parts, [whole(part) for part in parts], [out],
        [whole(out)], [], 1 << 20, 0, 5,
    )


def final_kernel(count, info, *refs):
    parts, far, (loss, pull) = refs[:count], refs[count:-2], refs[-2:]
    far = [parted_far(part[...]) for part in far]
    (target, (mass, cross)), (pred, (peak, total)) = joined(parts, far)
    pull[...] = target / mass - pred / total
    loss[...] = peak * log2 + jnp.log(total) - cross / mass / pred_temp


def finish(info, own, others):
    high, length = own[0].shape
    outs = [
        jax.ShapeDtypeStruct((1, length), jnp.float32),
        jax.ShapeDtypeStruct((high // len(names) - stat_rows, length), jnp.float32),
    ]
    ins = [*own, *others]
    return call(
        functools.partial(final_kernel, len(own)), "finish", info, (1,), ins,
        [whole(value) for value in ins], outs, [whole(out) for out in outs], [], 1 << 20, 0, 5,
    )[1:]


def swap(value, axis, bits):
    count = lax.axis_size(axis)
    return lax.ppermute(value, axis, [(i, i ^ bits) for i in range(count)])


def body(codes_view, pred_view, prototypes):
    rows = codes_view.shape[0]
    dp_count, proto_count = lax.axis_size("dp"), lax.axis_size("proto")
    z_count = dp_count // 2
    me, proto = lax.axis_index("dp"), lax.axis_index("proto")
    info = jnp.stack([me // 2, proto]).astype(jnp.int32)
    same_core = [[2 * z + core for z in range(z_count)] for core in range(2)]

    def sent(values):
        return [values[0]] + [swap(value, "proto", s) for s, value in enumerate(values[1:], 1)]

    protos = prototypes, swap(prototypes, "dp", 1)
    part = rows // proto_count
    piece = lax.dynamic_slice_in_dim(codes_view, proto * part, part, 0)
    quarters = [swap(piece, "dp", 2 * t) for t in range(1, z_count)]
    preds = lax.all_gather(pred_view, "dp", axis=0, tiled=True, axis_index_groups=same_core)

    info, stats, *protos = stats_part(info, [codes_view], protos, None)
    quarters, info = lax.optimization_barrier((quarters, info))
    quarters = jnp.stack(quarters)
    others = [swap(quarters, "proto", s) for s in range(1, proto_count)]
    info, *values = rows_part(info, None, pred_view, protos, None, rows, proto_count, 0, None)
    *earlier, near, across = values
    info, stats, *protos = stats_part(info, [quarters], (near, across), stats)
    info, stats, *protos = stats_part(info, others, protos, stats)
    codes = [quarters, *others]
    info, offset = offset_part(info, stats, swap(stats, "dp", 1))

    far, waiting = [], []
    for away in range(z_count - 1, 0, -1):
        info, *values = rows_part(
            info, codes, preds, protos, offset, rows, proto_count, away, None
        )
        *out, preds, near, across = values
        protos = near, across
        out = sent(out)
        for past, arrived in waiting:
            if far:
                far, arrived = lax.optimization_barrier((far, arrived))
            info, part = join_spread(info, arrived)
            far.append(swap(part, "dp", 2 * past))
        waiting = [(away, out)]
    info, *out = rows_part(
        info, codes_view, pred_view, protos, offset, rows, proto_count, 0, earlier
    )
    own = sent(out)
    ((past, arrived),) = waiting
    far, arrived = lax.optimization_barrier((far, arrived))
    info, part = join_spread(info, arrived)
    own, part = lax.optimization_barrier((own, part))
    loss, pull = finish(info, own, [*far, swap(part, "dp", 2 * past)])
    return (loss.reshape(rows), pull.T)


def solution(mesh):
    placed = (P("dp", None), P("dp", None), P(("proto", "dp"), None))
    return jax.shard_map(
        body, mesh=mesh, in_specs=placed, out_specs=(P("dp"), P("dp", "proto")), check_vma=False
    )
```

```python
import functools
import math

import jax
import jax.numpy as jnp
from jax import lax
from jax.experimental import pallas as pl
from jax.experimental.pallas import tpu as pltpu
from jax.sharding import PartitionSpec as P

code_temp = 0.05
pred_temp = 0.1
code_scale = math.log2(math.e) / code_temp
pred_scale = math.log2(math.e) / pred_temp
log2 = math.log(2.0)
stat_rows = 8
sent_rows = 16
low = -1e30
chunk = 512
mebi = 1024 * 1024


def scores(embeds, protos):
    return lax.dot_general(
        embeds, protos, (((1,), (1,)), ((), ())), preferred_element_type=jnp.float32
    )


def bare(value):
    return value.astype(jnp.bfloat16)


def add(parts):
    return functools.reduce(jnp.add, parts)


def lane_fold(combine, value):
    parts = [value[:, i : i + 128] for i in range(0, value.shape[1], 128)]
    return functools.reduce(combine, parts)


def padded(rows, width):
    filler = jnp.zeros((stat_rows - len(rows), width), jnp.float32)
    return jnp.concatenate([*rows, filler], axis=0)


def split_stats(stats):
    terms = []
    for row in stats:
        for _ in range(3):
            term = bare(row)
            row = row - term.astype(jnp.float32)
            terms.append(term)
    filler = jnp.zeros((sent_rows - len(terms), stats[0].shape[1]), jnp.bfloat16)
    return jnp.concatenate([*terms, filler], axis=0)


def join_stats(terms, count):
    wide = terms.astype(jnp.float32)
    return [add([wide[3 * i + j : 3 * i + j + 1] for j in range(3)]) for i in range(count)]


def parted(value):
    share = value.shape[0] - stat_rows
    return value[:share, :], [value[share + i : share + i + 1, :] for i in range(2)]


def parted_sent(value):
    share = value.shape[0] - sent_rows
    return value[:share, :].astype(jnp.float32), join_stats(value[share:, :], 2)


def packed(part):
    pull, stats = part
    return jnp.concatenate([pull, padded(stats, pull.shape[1])], axis=0)


def join_preds(parts):
    peak = functools.reduce(jnp.maximum, [stats[0] for _, stats in parts])
    factors = [jnp.exp2(stats[0] - peak) for _, stats in parts]
    pull = add([part * factor for (part, _), factor in zip(parts, factors)])
    total = add([stats[1] * factor for (_, stats), factor in zip(parts, factors)])
    return pull, [peak, total]


def join_targets(parts):
    stats = [add([stats[i] for _, stats in parts]) for i in range(2)]
    return add([part for part, _ in parts]), stats


joins = {"pred": join_preds, "target": join_targets}


def send(info, place, pull, stats, outs, flipped):
    kept, *sent = outs
    share = pull.shape[1] // len(outs)
    high, tall = share + stat_rows, share + sent_rows
    flipped[...] = pull.T
    mine = pl.multiple_of(info[1] * share, share)
    kept[place * high : place * high + share, :] = flipped[pl.ds(mine, share), :]
    kept[place * high + share : (place + 1) * high, :] = padded(stats, pull.shape[0])
    terms = split_stats(stats)
    for s, out in enumerate(sent, 1):
        start = pl.multiple_of((info[1] ^ s) * share, share)
        out[place * tall : place * tall + share, :] = bare(flipped[pl.ds(start, share), :])
        out[place * tall + share : (place + 1) * tall, :] = terms


def whole(value):
    return pl.BlockSpec(value.shape, lambda *_: (0,) * len(value.shape))


def call(kernel, name, info, grid, ins, in_specs, outs, out_specs, scratch, flops, exps, room, passed=()):
    count, total = len(ins), len(ins) + len(outs)

    def without(*refs):
        return kernel(*refs[: 1 + total], *refs[1 + total + len(passed) :])

    outs = [*outs, *[jax.ShapeDtypeStruct(ins[i].shape, ins[i].dtype) for i in passed]]
    out_specs = [*out_specs, *[pl.BlockSpec(memory_space=pl.ANY)] * len(passed)]
    values = pl.pallas_call(
        without,
        grid_spec=pltpu.PrefetchScalarGridSpec(
            num_scalar_prefetch=1,
            grid=grid,
            in_specs=in_specs,
            out_specs=out_specs,
            scratch_shapes=scratch,
        ),
        out_shape=outs,
        input_output_aliases={1 + i: total - count + k for k, i in enumerate(passed)},
        compiler_params=pltpu.CompilerParams(vmem_limit_bytes=room * mebi),
        cost_estimate=pl.CostEstimate(flops=flops, bytes_accessed=flops // 128, transcendentals=exps),
        name=name,
    )(info, *ins)
    info, first = lax.optimization_barrier((info, values[0]))
    return info, first, *values[1:]


def placed_rows(info, quarters, block):
    part = quarters[0].shape[1]
    for s, quarter in enumerate(quarters):
        place = pl.multiple_of((info[1] ^ s) * part, part)
        block[pl.ds(place, part), :] = quarter[0]


def over_chunks(protos, width, step, unrolled=False):
    count = protos[0].shape[0] // width
    if unrolled:
        for i in range(count):
            for half, part in enumerate(protos):
                step(half * count + i, part[i * width : (i + 1) * width, :])
        return

    def both(i, carry):
        at = pl.ds(pl.multiple_of(i * width, width), width)
        for half, part in enumerate(protos):
            step(half * count + i, part[at, :])
        return carry

    lax.fori_loop(0, count, both, 0)


def stats_kernel(fresh, info, *refs):
    if fresh:
        *codes, near, across, stats, copied = refs
        copied[...] = near[...]
        stats[:, 0:1, :] = jnp.full((stats.shape[0], 1, stats.shape[2]), low, jnp.float32)
        stats[:, 1:, :] = jnp.zeros((stats.shape[0], stat_rows - 1, stats.shape[2]), jnp.float32)
    else:
        *codes, near, across, before, stats = refs
        stats[...] = before[...]
    for part in codes:
        rows = part[...].reshape(-1, part.shape[-1])

        def step(j, protos):
            raw = scores(rows, protos)
            old, total = stats[j, 0:1, :], stats[j, 1:2, :]
            new = jnp.maximum(old, jnp.max(raw, axis=0, keepdims=True))
            value = jnp.exp2((raw - new) * code_scale)
            stats[j, 1:2, :] = total * jnp.exp2((old - new) * code_scale) + jnp.sum(
                value, axis=0, keepdims=True
            )
            stats[j, 0:1, :] = new

        over_chunks((near, across), stats.shape[2], step, True)


def stats_part(info, codes, protos, before):
    count, dim = protos[0].shape
    width = min(chunk, count)
    rows = sum(math.prod(part.shape[:-1]) for part in codes)
    outs = [jax.ShapeDtypeStruct((2 * count // width, stat_rows, width), jnp.float32)]
    ins, passed = [*codes, *protos], [len(codes), len(codes) + 1]
    if before is None:
        outs.append(jax.ShapeDtypeStruct(protos[0].shape, protos[0].dtype))
        passed = passed[1:]
    else:
        ins.append(before)
    return call(
        functools.partial(stats_kernel, before is None), "stats_part", info, (1,), ins,
        [whole(value) for value in ins], outs, [whole(out) for out in outs], [],
        4 * rows * count * dim, 2 * rows * count, 6, passed,
    )


def offset_kernel(info, stats, other, out):
    count = stats.shape[0] // 2
    for j in range(2 * count):
        here, there = stats[j], other[(j + count) % (2 * count)]
        peak = jnp.maximum(here[0:1], there[0:1])
        mass = here[1:2] * jnp.exp2((here[0:1] - peak) * code_scale) + there[1:2] * jnp.exp2(
            (there[0:1] - peak) * code_scale
        )
        offset = peak * code_scale + jnp.log2(mass)
        out[j] = jnp.broadcast_to(offset, out.shape[1:])


def offset_part(info, stats, other):
    return call(
        offset_kernel, "offset_part", info, (1,), [stats, other], [whole(stats)] * 2, [stats],
        [whole(stats)], [], 1 << 20, 0, 5,
    )


def weighted(value, protos):
    return jnp.dot(bare(value), protos, preferred_element_type=jnp.float32)


def row_of(combine, value):
    return combine(value.T, axis=0, keepdims=True)


def pred_logits(preds, protos, raws, top, j):
    raw = scores(preds[...], protos)
    raws[j] = raw
    top[...] = jnp.maximum(top[...], lane_fold(jnp.maximum, raw))


def pred_pull(protos, raws, top, total, pull):
    width = raws.shape[2]
    stats = [row_of(jnp.max, top[...]) * pred_scale]
    peak = jnp.max(top[...], axis=1, keepdims=True)
    top[...] = jnp.broadcast_to(peak, top.shape)
    total[...] = jnp.zeros(total.shape, jnp.float32)
    pull[...] = jnp.zeros(pull.shape, jnp.float32)

    def step(j, protos):
        peak = jnp.concatenate([top[...]] * (width // 128), axis=1)
        value = jnp.exp2((raws[j] - peak) * pred_scale)
        total[...] += lane_fold(jnp.add, value)
        pull[...] += weighted(value, protos)

    over_chunks(protos, width, step)
    return pull[...], [*stats, row_of(jnp.sum, total[...])]


def target_step(codes, protos, offset, total, pull, j):
    value = jnp.exp2(scores(codes[...], protos) * code_scale - offset[j, 0:1, :])
    total[...] += lane_fold(jnp.add, value)
    pull[...] += weighted(value, protos)


def target_stats(preds, total, pull):
    cross = lane_fold(jnp.add, pull[...] * preds[...].astype(jnp.float32))
    return [row_of(jnp.sum, total[...]), row_of(jnp.sum, cross)]


def pred_kernel(info, preds, near, across, *refs):
    *outs, raws, top, total, pull, flipped = refs
    protos = near, across
    top[...] = jnp.full(top.shape, low, jnp.float32)
    over_chunks(protos, raws.shape[2], lambda j, part: pred_logits(preds, part, raws, top, j))
    send(info, 0, *pred_pull(protos, raws, top, total, pull), outs, flipped)


def target_kernel(info, codes, preds, near, across, offset, *refs):
    *refs, total, pull, flipped = refs
    earlier, outs = refs[: len(refs) // 2], refs[len(refs) // 2 :]
    total[...] = jnp.zeros(total.shape, jnp.float32)
    pull[...] = jnp.zeros(pull.shape, jnp.float32)
    over_chunks(
        (near, across),
        offset.shape[2],
        lambda j, part: target_step(codes, part, offset, total, pull, j),
        True,
    )
    send(info, 0, pull[...], target_stats(preds, total, pull), outs, flipped)
    for part, out in zip(earlier, outs):
        out[part.shape[0] :, :] = part[...]


def both_kernel(proto_count, info, *refs):
    near, across, offset = refs[2 * proto_count : 2 * proto_count + 3]
    outs = refs[2 * proto_count + 3 : -7]
    raws, top, total, pull, flipped, codes, preds = refs[-7:]
    protos = near, across
    placed_rows(info, refs[:proto_count], codes)
    placed_rows(info, refs[proto_count : 2 * proto_count], preds)
    top[...] = jnp.full(top.shape, low, jnp.float32)
    total[...] = jnp.zeros(total.shape, jnp.float32)
    pull[...] = jnp.zeros(pull.shape, jnp.float32)

    def step(j, part):
        pred_logits(preds, part, raws, top, j)
        target_step(codes, part, offset, total, pull, j)

    over_chunks(protos, offset.shape[2], step)
    send(info, 0, pull[...], target_stats(preds, total, pull), outs, flipped)
    send(info, 1, *pred_pull(protos, raws, top, total, pull), outs, flipped)


def rows_part(info, codes, preds, protos, offset, rows, proto_count, away, earlier):
    count, dim = protos[0].shape
    share = dim // proto_count
    width = min(chunk, count)
    shapes = [(2 * count // width, rows, width), (rows, 128), (rows, 128), (rows, dim), (dim, rows)]
    scratch = [pltpu.VMEM(shape, jnp.float32) for shape in shapes]
    if codes is None:
        kernel, ins, passed = pred_kernel, [preds, *protos], (1, 2)
        specs = [whole(value) for value in ins]
    elif not away:
        kernel, ins, passed = target_kernel, [codes, preds, *protos, offset, *earlier], ()
        specs, scratch = [whole(value) for value in ins], scratch[2:]
    else:
        kernel, ins = functools.partial(both_kernel, proto_count), [*codes, *preds, *protos, offset]
        passed = tuple(2 * proto_count + i for i in range(2))
        quarter = pl.BlockSpec((1, *codes[0].shape[1:]), lambda i, info: (away - 1, 0, 0))
        specs = [quarter] * (2 * proto_count) + [whole(value) for value in ins[-3:]]
        scratch = [*scratch] + [pltpu.VMEM((rows, dim), jnp.bfloat16)] * 2
    parts, work = 2 if codes is not None else 1, 2 if away else 1
    high, tall = parts * (share + stat_rows), parts * (share + sent_rows)
    outs = [jax.ShapeDtypeStruct((high, rows), jnp.float32)]
    outs += [jax.ShapeDtypeStruct((tall, rows), jnp.bfloat16)] * (proto_count - 1)
    return call(
        kernel, "rows_part", info, (1,), ins, specs, outs, [whole(out) for out in outs], scratch,
        work * 8 * rows * count * dim, work * 2 * rows * count,
        6 if kernel is target_kernel else 14, passed,
    )


names = ["target", "pred"]


def packed_far(target, pred):
    pull, stats = pred
    high = bare(pull)
    rest = bare(pull - high.astype(jnp.float32))
    return jnp.concatenate([bare(target[0]), high, rest, split_stats([*target[1], *stats])], axis=0)


def parted_far(value):
    share = (value.shape[0] - sent_rows) // 3
    target, high, rest = [
        value[i * share : (i + 1) * share, :].astype(jnp.float32) for i in range(3)
    ]
    stats = join_stats(value[3 * share :, :], 4)
    return {"target": (target, stats[:2]), "pred": (high + rest, stats[2:])}


def joined(parts, others=()):
    kept, *sent = parts
    high, tall = kept.shape[0] // len(names), sent[0].shape[0] // len(names)
    return [
        joins[name](
            [parted(kept[i * high : (i + 1) * high, :])]
            + [parted_sent(part[i * tall : (i + 1) * tall, :]) for part in sent]
            + [part[name] for part in others]
        )
        for i, name in enumerate(names)
    ]


def spread_kernel(info, *refs):
    *parts, out = refs
    out[...] = packed_far(*joined(parts))


def join_spread(info, parts):
    high, rows = parts[0].shape
    share = high // len(names) - stat_rows
    out = jax.ShapeDtypeStruct((3 * share + sent_rows, rows), jnp.bfloat16)
    return call(
        spread_kernel, "join_spread", info, (1,), parts, [whole(part) for part in parts], [out],
        [whole(out)], [], 1 << 20, 0, 5,
    )


def final_kernel(count, info, *refs):
    parts, far, (loss, pull) = refs[:count], refs[count:-2], refs[-2:]
    far = [parted_far(part[...]) for part in far]
    (target, (mass, cross)), (pred, (peak, total)) = joined(parts, far)
    pull[...] = target / mass - pred / total
    loss[...] = peak * log2 + jnp.log(total) - cross / mass / pred_temp


def finish(info, own, others):
    high, length = own[0].shape
    outs = [
        jax.ShapeDtypeStruct((1, length), jnp.float32),
        jax.ShapeDtypeStruct((high // len(names) - stat_rows, length), jnp.float32),
    ]
    ins = [*own, *others]
    return call(
        functools.partial(final_kernel, len(own)), "finish", info, (1,), ins,
        [whole(value) for value in ins], outs, [whole(out) for out in outs], [], 1 << 20, 0, 5,
    )[1:]


def swap(value, axis, bits):
    count = lax.axis_size(axis)
    return lax.ppermute(value, axis, [(i, i ^ bits) for i in range(count)])


def body(codes_view, pred_view, prototypes):
    rows = codes_view.shape[0]
    dp_count, proto_count = lax.axis_size("dp"), lax.axis_size("proto")
    z_count = dp_count // 2
    me, proto = lax.axis_index("dp"), lax.axis_index("proto")
    info = jnp.stack([me // 2, proto]).astype(jnp.int32)

    def sent(values):
        return [values[0]] + [swap(value, "proto", s) for s, value in enumerate(values[1:], 1)]

    protos = prototypes, swap(prototypes, "dp", 1)
    part = rows // proto_count
    piece = jnp.concatenate(
        [
            lax.dynamic_slice_in_dim(view, proto * part, part, 0)
            for view in (codes_view, pred_view)
        ]
    )
    quarters = [swap(piece, "dp", 2 * t) for t in range(1, z_count)]

    def around(value):
        return [value] + [swap(value, "proto", s) for s in range(1, proto_count)]

    info, stats, *protos = stats_part(info, [codes_view], protos, None)
    info, *values = rows_part(info, None, pred_view, protos, None, rows, proto_count, 0, None)
    *earlier, near, across = values
    quarters, info = lax.optimization_barrier((quarters, info))
    codes = around(jnp.stack([value[:part] for value in quarters]))
    preds = jnp.stack([value[part:] for value in quarters])
    info, stats, *protos = stats_part(info, codes[:1], (near, across), stats)
    preds, info = lax.optimization_barrier((preds, info))
    preds = around(preds)
    info, stats, *protos = stats_part(info, codes[1:], protos, stats)
    info, offset = offset_part(info, stats, swap(stats, "dp", 1))

    far, waiting = [], []
    for away in range(z_count - 1, 0, -1):
        info, *values = rows_part(
            info, codes, preds, protos, offset, rows, proto_count, away, None
        )
        *out, near, across = values
        protos = near, across
        out = sent(out)
        for past, arrived in waiting:
            if far:
                far, arrived = lax.optimization_barrier((far, arrived))
            info, part = join_spread(info, arrived)
            far.append(swap(part, "dp", 2 * past))
        waiting = [(away, out)]
    info, *out = rows_part(
        info, codes_view, pred_view, protos, offset, rows, proto_count, 0, earlier
    )
    own = sent(out)
    ((past, arrived),) = waiting
    far, arrived = lax.optimization_barrier((far, arrived))
    info, part = join_spread(info, arrived)
    loss, pull = finish(info, own, [*far, swap(part, "dp", 2 * past)])
    return (loss.reshape(rows), pull.T)


def solution(mesh):
    placed = (P("dp", None), P("dp", None), P(("proto", "dp"), None))
    return jax.shard_map(
        body, mesh=mesh, in_specs=placed, out_specs=(P("dp"), P("dp", "proto")), check_vma=False
    )
```

```python
import functools
import math

import jax
import jax.numpy as jnp
from jax import lax
from jax.experimental import pallas as pl
from jax.experimental.pallas import tpu as pltpu
from jax.sharding import PartitionSpec as P

code_temp = 0.05
pred_temp = 0.1
code_scale = math.log2(math.e) / code_temp
pred_scale = math.log2(math.e) / pred_temp
log2 = math.log(2.0)
too_large = 2.0**100
stat_rows = 8
sent_rows = 16
low = -1e30
chunk = 512
mebi = 1024 * 1024


def scores(embeds, protos):
    return lax.dot_general(
        embeds, protos, (((1,), (1,)), ((), ())), preferred_element_type=jnp.float32
    )


def bare(value):
    return value.astype(jnp.bfloat16)


def add(parts):
    return functools.reduce(jnp.add, parts)


def lane_fold(combine, value):
    parts = [value[:, i : i + 128] for i in range(0, value.shape[1], 128)]
    return functools.reduce(combine, parts)


def padded(rows, width):
    filler = jnp.zeros((stat_rows - len(rows), width), jnp.float32)
    return jnp.concatenate([*rows, filler], axis=0)


def split_stats(stats):
    terms = []
    for row in stats:
        for _ in range(3):
            term = bare(row)
            row = row - term.astype(jnp.float32)
            terms.append(term)
    filler = jnp.zeros((sent_rows - len(terms), stats[0].shape[1]), jnp.bfloat16)
    return jnp.concatenate([*terms, filler], axis=0)


def join_stats(terms, count):
    wide = terms.astype(jnp.float32)
    return [add([wide[3 * i + j : 3 * i + j + 1] for j in range(3)]) for i in range(count)]


def parted(value):
    share = value.shape[0] - stat_rows
    return value[:share, :], [value[share + i : share + i + 1, :] for i in range(2)]


def parted_sent(value):
    share = value.shape[0] - sent_rows
    return value[:share, :].astype(jnp.float32), join_stats(value[share:, :], 2)


def packed(part):
    pull, stats = part
    return jnp.concatenate([pull, padded(stats, pull.shape[1])], axis=0)


def join_preds(parts):
    peak = functools.reduce(jnp.maximum, [stats[0] for _, stats in parts])
    factors = [jnp.exp2(stats[0] - peak) for _, stats in parts]
    pull = add([part * factor for (part, _), factor in zip(parts, factors)])
    total = add([stats[1] * factor for (_, stats), factor in zip(parts, factors)])
    return pull, [peak, total]


def join_targets(parts):
    stats = [add([stats[i] for _, stats in parts]) for i in range(2)]
    return add([part for part, _ in parts]), stats


joins = {"pred": join_preds, "target": join_targets}


def send(info, place, pull, stats, outs, flipped):
    kept, *sent = outs
    share = pull.shape[1] // len(outs)
    high, tall = share + stat_rows, share + sent_rows
    flipped[...] = pull.T
    mine = pl.multiple_of(info[1] * share, share)
    kept[place * high : place * high + share, :] = flipped[pl.ds(mine, share), :]
    kept[place * high + share : (place + 1) * high, :] = padded(stats, pull.shape[0])
    terms = split_stats(stats)
    for s, out in enumerate(sent, 1):
        start = pl.multiple_of((info[1] ^ s) * share, share)
        out[place * tall : place * tall + share, :] = bare(flipped[pl.ds(start, share), :])
        out[place * tall + share : (place + 1) * tall, :] = terms


def whole(value):
    return pl.BlockSpec(value.shape, lambda *_: (0,) * len(value.shape))


def call(kernel, name, info, grid, ins, in_specs, outs, out_specs, scratch, flops, exps, room, passed=()):
    count, total = len(ins), len(ins) + len(outs)

    def without(*refs):
        return kernel(*refs[: 1 + total], *refs[1 + total + len(passed) :])

    outs = [*outs, *[jax.ShapeDtypeStruct(ins[i].shape, ins[i].dtype) for i in passed]]
    out_specs = [*out_specs, *[pl.BlockSpec(memory_space=pl.ANY)] * len(passed)]
    values = pl.pallas_call(
        without,
        grid_spec=pltpu.PrefetchScalarGridSpec(
            num_scalar_prefetch=1,
            grid=grid,
            in_specs=in_specs,
            out_specs=out_specs,
            scratch_shapes=scratch,
        ),
        out_shape=outs,
        input_output_aliases={1 + i: total - count + k for k, i in enumerate(passed)},
        compiler_params=pltpu.CompilerParams(vmem_limit_bytes=room * mebi),
        cost_estimate=pl.CostEstimate(flops=flops, bytes_accessed=flops // 128, transcendentals=exps),
        name=name,
    )(info, *ins)
    info, first = lax.optimization_barrier((info, values[0]))
    return info, first, *values[1:]


def placed_rows(info, quarters, block):
    part = quarters[0].shape[1]
    for s, quarter in enumerate(quarters):
        place = pl.multiple_of((info[1] ^ s) * part, part)
        block[pl.ds(place, part), :] = quarter[0]


def over_chunks(protos, width, step, unrolled=False):
    count = protos[0].shape[0] // width
    if unrolled:
        for i in range(count):
            for half, part in enumerate(protos):
                step(half * count + i, part[i * width : (i + 1) * width, :])
        return

    def both(i, carry):
        at = pl.ds(pl.multiple_of(i * width, width), width)
        for half, part in enumerate(protos):
            step(half * count + i, part[at, :])
        return carry

    lax.fori_loop(0, count, both, 0)


def column_sums(raw, peak):
    return jnp.sum(jnp.exp2((raw - peak) * code_scale), axis=0, keepdims=True)


def stats_kernel(fresh, info, *refs):
    if fresh:
        *codes, near, across, stats, copied = refs
        copied[...] = near[...]
    else:
        *codes, near, across, before, stats = refs
        stats[...] = before[...]
    protos, width = (near, across), stats.shape[2]

    def first(j, part):
        raw = scores(codes[0][...], part)
        peak = jnp.max(raw, axis=0, keepdims=True)
        stats[j, 0:1, :] = peak
        stats[j, 1:2, :] = column_sums(raw, peak)

    def kept_peak(rows, j, part):
        stats[j, 1:2, :] += column_sums(scores(rows, part), stats[j, 0:1, :])

    def new_peak(rows, j, part):
        raw = scores(rows, part)
        old, total = stats[j, 0:1, :], stats[j, 1:2, :]
        peak = jnp.maximum(old, jnp.max(raw, axis=0, keepdims=True))
        stats[j, 0:1, :] = peak
        stats[j, 1:2, :] = total * jnp.exp2((old - peak) * code_scale) + column_sums(raw, peak)

    def all_rows(add_rows, unrolled):
        for part in codes:
            rows = part[...].reshape(-1, part.shape[-1])
            over_chunks(protos, width, functools.partial(add_rows, rows), unrolled)

    if fresh:
        over_chunks(protos, width, first, True)
        return
    all_rows(kept_peak, True)
    worst = jnp.max(stats[:, 1:2, :])

    @pl.when(jnp.logical_not(worst < too_large))
    def _():
        stats[...] = before[...]
        all_rows(new_peak, False)


def stats_part(info, codes, protos, before):
    count, dim = protos[0].shape
    width = min(chunk, count)
    rows = sum(math.prod(part.shape[:-1]) for part in codes)
    outs = [jax.ShapeDtypeStruct((2 * count // width, stat_rows, width), jnp.float32)]
    ins, passed = [*codes, *protos], [len(codes), len(codes) + 1]
    if before is None:
        outs.append(jax.ShapeDtypeStruct(protos[0].shape, protos[0].dtype))
        passed = passed[1:]
    else:
        ins.append(before)
    return call(
        functools.partial(stats_kernel, before is None), "stats_part", info, (1,), ins,
        [whole(value) for value in ins], outs, [whole(out) for out in outs], [],
        4 * rows * count * dim, 2 * rows * count, 6, passed,
    )


def offset_kernel(info, stats, other, out):
    count = stats.shape[0] // 2
    for j in range(2 * count):
        here, there = stats[j], other[(j + count) % (2 * count)]
        peak = jnp.maximum(here[0:1], there[0:1])
        mass = here[1:2] * jnp.exp2((here[0:1] - peak) * code_scale) + there[1:2] * jnp.exp2(
            (there[0:1] - peak) * code_scale
        )
        offset = peak * code_scale + jnp.log2(mass)
        out[j] = jnp.broadcast_to(offset, out.shape[1:])


def offset_part(info, stats, other):
    return call(
        offset_kernel, "offset_part", info, (1,), [stats, other], [whole(stats)] * 2, [stats],
        [whole(stats)], [], 1 << 20, 0, 5,
    )


def weighted(value, protos):
    return jnp.dot(bare(value), protos, preferred_element_type=jnp.float32)


def row_of(combine, value):
    return combine(value.T, axis=0, keepdims=True)


def pred_logits(preds, protos, raws, top, j):
    raw = scores(preds[...], protos)
    raws[j] = raw
    top[...] = jnp.maximum(top[...], lane_fold(jnp.maximum, raw))


def pred_pull(protos, raws, top, total, pull, beside=None):
    width = raws.shape[2]
    stats = [row_of(jnp.max, top[...]) * pred_scale]
    peak = jnp.max(top[...], axis=1, keepdims=True)
    top[...] = jnp.broadcast_to(peak, top.shape)
    total[...] = jnp.zeros(total.shape, jnp.float32)
    pull[...] = jnp.zeros(pull.shape, jnp.float32)

    def step(j, protos):
        peak = jnp.concatenate([top[...]] * (width // 128), axis=1)
        value = jnp.exp2((raws[j] - peak) * pred_scale)
        total[...] += lane_fold(jnp.add, value)
        pull[...] += weighted(value, protos)
        if beside is not None:
            beside(j, protos)

    over_chunks(protos, width, step)
    return pull[...], [*stats, row_of(jnp.sum, total[...])]


def target_values(codes, protos, offset, total, j):
    value = jnp.exp2(scores(codes[...], protos) * code_scale - offset[j, 0:1, :])
    total[...] += lane_fold(jnp.add, value)
    return value


def target_step(codes, protos, offset, total, pull, j):
    pull[...] += weighted(target_values(codes, protos, offset, total, j), protos)


def target_stats(preds, total, pull):
    cross = lane_fold(jnp.add, pull[...] * preds[...].astype(jnp.float32))
    return [row_of(jnp.sum, total[...]), row_of(jnp.sum, cross)]


def pred_kernel(info, preds, near, across, *refs):
    *outs, raws, top, total, pull, flipped = refs
    protos = near, across
    top[...] = jnp.full(top.shape, low, jnp.float32)
    over_chunks(protos, raws.shape[2], lambda j, part: pred_logits(preds, part, raws, top, j))
    send(info, 0, *pred_pull(protos, raws, top, total, pull), outs, flipped)


def target_kernel(info, codes, preds, near, across, offset, *refs):
    *refs, total, pull, flipped = refs
    earlier, outs = refs[: len(refs) // 2], refs[len(refs) // 2 :]
    total[...] = jnp.zeros(total.shape, jnp.float32)
    pull[...] = jnp.zeros(pull.shape, jnp.float32)
    over_chunks(
        (near, across),
        offset.shape[2],
        lambda j, part: target_step(codes, part, offset, total, pull, j),
        True,
    )
    send(info, 0, pull[...], target_stats(preds, total, pull), outs, flipped)
    for part, out in zip(earlier, outs):
        out[part.shape[0] :, :] = part[...]


def both_kernel(proto_count, info, *refs):
    near, across, offset = refs[2 * proto_count : 2 * proto_count + 3]
    outs = refs[2 * proto_count + 3 : -10]
    raws, top, total, pull, flipped, codes, preds, held, pull_pred, total_pred = refs[-10:]
    protos = near, across
    placed_rows(info, refs[:proto_count], codes)
    placed_rows(info, refs[proto_count : 2 * proto_count], preds)
    top[...] = jnp.full(top.shape, low, jnp.float32)
    total[...] = jnp.zeros(total.shape, jnp.float32)
    pull[...] = jnp.zeros(pull.shape, jnp.float32)

    def step(j, part):
        pred_logits(preds, part, raws, top, j)
        held[j] = bare(target_values(codes, part, offset, total, j))

    def beside(j, part):
        pull[...] += jnp.dot(held[j], part, preferred_element_type=jnp.float32)

    over_chunks(protos, offset.shape[2], step)
    done = pred_pull(protos, raws, top, total_pred, pull_pred, beside)
    send(info, 0, pull[...], target_stats(preds, total, pull), outs, flipped)
    send(info, 1, *done, outs, flipped)


def rows_part(info, codes, preds, protos, offset, rows, proto_count, away, earlier):
    count, dim = protos[0].shape
    share = dim // proto_count
    width = min(chunk, count)
    shapes = [(2 * count // width, rows, width), (rows, 128), (rows, 128), (rows, dim), (dim, rows)]
    scratch = [pltpu.VMEM(shape, jnp.float32) for shape in shapes]
    if codes is None:
        kernel, ins, passed = pred_kernel, [preds, *protos], (1, 2)
        specs = [whole(value) for value in ins]
    elif not away:
        kernel, ins, passed = target_kernel, [codes, preds, *protos, offset, *earlier], ()
        specs, scratch = [whole(value) for value in ins], scratch[2:]
    else:
        kernel, ins = functools.partial(both_kernel, proto_count), [*codes, *preds, *protos, offset]
        passed = tuple(2 * proto_count + i for i in range(2))
        quarter = pl.BlockSpec((1, *codes[0].shape[1:]), lambda i, info: (away - 1, 0, 0))
        specs = [quarter] * (2 * proto_count) + [whole(value) for value in ins[-3:]]
        scratch = [*scratch] + [pltpu.VMEM((rows, dim), jnp.bfloat16)] * 2
        scratch += [pltpu.VMEM(shapes[0], jnp.bfloat16)]
        scratch += [pltpu.VMEM(shape, jnp.float32) for shape in ((rows, dim), (rows, 128))]
    parts, work = 2 if codes is not None else 1, 2 if away else 1
    high, tall = parts * (share + stat_rows), parts * (share + sent_rows)
    outs = [jax.ShapeDtypeStruct((high, rows), jnp.float32)]
    outs += [jax.ShapeDtypeStruct((tall, rows), jnp.bfloat16)] * (proto_count - 1)
    return call(
        kernel, "rows_part", info, (1,), ins, specs, outs, [whole(out) for out in outs], scratch,
        work * 8 * rows * count * dim, work * 2 * rows * count,
        6 if kernel is target_kernel else 20, passed,
    )


names = ["target", "pred"]


def packed_far(target, pred):
    pull, stats = pred
    high = bare(pull)
    rest = bare(pull - high.astype(jnp.float32))
    return jnp.concatenate([bare(target[0]), high, rest, split_stats([*target[1], *stats])], axis=0)


def parted_far(value):
    share = (value.shape[0] - sent_rows) // 3
    target, high, rest = [
        value[i * share : (i + 1) * share, :].astype(jnp.float32) for i in range(3)
    ]
    stats = join_stats(value[3 * share :, :], 4)
    return {"target": (target, stats[:2]), "pred": (high + rest, stats[2:])}


def joined(parts, others=()):
    kept, *sent = parts
    high, tall = kept.shape[0] // len(names), sent[0].shape[0] // len(names)
    return [
        joins[name](
            [parted(kept[i * high : (i + 1) * high, :])]
            + [parted_sent(part[i * tall : (i + 1) * tall, :]) for part in sent]
            + [part[name] for part in others]
        )
        for i, name in enumerate(names)
    ]


def spread_kernel(info, *refs):
    *parts, out = refs
    out[...] = packed_far(*joined(parts))


def join_spread(info, parts):
    high, rows = parts[0].shape
    share = high // len(names) - stat_rows
    out = jax.ShapeDtypeStruct((3 * share + sent_rows, rows), jnp.bfloat16)
    return call(
        spread_kernel, "join_spread", info, (1,), parts, [whole(part) for part in parts], [out],
        [whole(out)], [], 1 << 20, 0, 5,
    )


def final_kernel(count, info, *refs):
    parts, far, (loss, pull) = refs[:count], refs[count:-2], refs[-2:]
    far = [parted_far(part[...]) for part in far]
    (target, (mass, cross)), (pred, (peak, total)) = joined(parts, far)
    pull[...] = target / mass - pred / total
    loss[...] = peak * log2 + jnp.log(total) - cross / mass / pred_temp


def finish(info, own, others):
    high, length = own[0].shape
    outs = [
        jax.ShapeDtypeStruct((1, length), jnp.float32),
        jax.ShapeDtypeStruct((high // len(names) - stat_rows, length), jnp.float32),
    ]
    ins = [*own, *others]
    return call(
        functools.partial(final_kernel, len(own)), "finish", info, (1,), ins,
        [whole(value) for value in ins], outs, [whole(out) for out in outs], [], 1 << 20, 0, 5,
    )[1:]


def swap(value, axis, bits):
    count = lax.axis_size(axis)
    return lax.ppermute(value, axis, [(i, i ^ bits) for i in range(count)])


def body(codes_view, pred_view, prototypes):
    rows = codes_view.shape[0]
    dp_count, proto_count = lax.axis_size("dp"), lax.axis_size("proto")
    z_count = dp_count // 2
    me, proto = lax.axis_index("dp"), lax.axis_index("proto")
    info = jnp.stack([me // 2, proto]).astype(jnp.int32)

    def sent(values):
        return [values[0]] + [swap(value, "proto", s) for s, value in enumerate(values[1:], 1)]

    protos = prototypes, swap(prototypes, "dp", 1)
    part = rows // proto_count
    piece = jnp.concatenate(
        [
            lax.dynamic_slice_in_dim(view, proto * part, part, 0)
            for view in (codes_view, pred_view)
        ]
    )
    quarters = [swap(piece, "dp", 2 * t) for t in range(1, z_count)]

    def around(value):
        return [value] + [swap(value, "proto", s) for s in range(1, proto_count)]

    info, stats, *protos = stats_part(info, [codes_view], protos, None)
    info, *values = rows_part(info, None, pred_view, protos, None, rows, proto_count, 0, None)
    *earlier, near, across = values
    quarters, info = lax.optimization_barrier((quarters, info))
    codes = around(jnp.stack([value[:part] for value in quarters]))
    preds = jnp.stack([value[part:] for value in quarters])
    info, stats, *protos = stats_part(info, codes[:1], (near, across), stats)
    preds, info = lax.optimization_barrier((preds, info))
    preds = around(preds)
    info, stats, *protos = stats_part(info, codes[1:], protos, stats)
    info, offset = offset_part(info, stats, swap(stats, "dp", 1))

    far, waiting = [], []
    for away in range(z_count - 1, 0, -1):
        info, *values = rows_part(
            info, codes, preds, protos, offset, rows, proto_count, away, None
        )
        *out, near, across = values
        protos = near, across
        out = sent(out)
        for past, arrived in waiting:
            if far:
                far, arrived = lax.optimization_barrier((far, arrived))
            info, part = join_spread(info, arrived)
            far.append(swap(part, "dp", 2 * past))
        waiting = [(away, out)]
    info, *out = rows_part(
        info, codes_view, pred_view, protos, offset, rows, proto_count, 0, earlier
    )
    own = sent(out)
    ((past, arrived),) = waiting
    far, arrived = lax.optimization_barrier((far, arrived))
    info, part = join_spread(info, arrived)
    loss, pull = finish(info, own, [*far, swap(part, "dp", 2 * past)])
    return (loss.reshape(rows), pull.T)


def solution(mesh):
    placed = (P("dp", None), P("dp", None), P(("proto", "dp"), None))
    return jax.shard_map(
        body, mesh=mesh, in_specs=placed, out_specs=(P("dp"), P("dp", "proto")), check_vma=False
    )
```

```python
import functools
import math

import jax
import jax.numpy as jnp
from jax import lax
from jax.experimental import pallas as pl
from jax.experimental.pallas import tpu as pltpu
from jax.sharding import PartitionSpec as P

code_temp = 0.05
pred_temp = 0.1
code_scale = math.log2(math.e) / code_temp
pred_scale = math.log2(math.e) / pred_temp
log2 = math.log(2.0)
too_large = 2.0**100
stat_rows = 8
sent_rows = 16
low = -1e30
chunk = 512
mebi = 1024 * 1024


def scores(embeds, protos):
    return lax.dot_general(
        embeds, protos, (((1,), (1,)), ((), ())), preferred_element_type=jnp.float32
    )


def bare(value):
    return value.astype(jnp.bfloat16)


def add(parts):
    return functools.reduce(jnp.add, parts)


def lane_fold(combine, value):
    parts = [value[:, i : i + 128] for i in range(0, value.shape[1], 128)]
    return functools.reduce(combine, parts)


def padded(rows, width):
    filler = jnp.zeros((stat_rows - len(rows), width), jnp.float32)
    return jnp.concatenate([*rows, filler], axis=0)


def split_stats(stats):
    terms = []
    for row in stats:
        for _ in range(3):
            term = bare(row)
            row = row - term.astype(jnp.float32)
            terms.append(term)
    filler = jnp.zeros((sent_rows - len(terms), stats[0].shape[1]), jnp.bfloat16)
    return jnp.concatenate([*terms, filler], axis=0)


def join_stats(terms, count):
    wide = terms.astype(jnp.float32)
    return [add([wide[3 * i + j : 3 * i + j + 1] for j in range(3)]) for i in range(count)]


def parted(value):
    share = value.shape[0] - stat_rows
    return value[:share, :], [value[share + i : share + i + 1, :] for i in range(2)]


def parted_sent(value):
    share = value.shape[0] - sent_rows
    return value[:share, :].astype(jnp.float32), join_stats(value[share:, :], 2)


def packed(part):
    pull, stats = part
    return jnp.concatenate([pull, padded(stats, pull.shape[1])], axis=0)


def join_preds(parts):
    peak = functools.reduce(jnp.maximum, [stats[0] for _, stats in parts])
    factors = [jnp.exp2(stats[0] - peak) for _, stats in parts]
    pull = add([part * factor for (part, _), factor in zip(parts, factors)])
    total = add([stats[1] * factor for (_, stats), factor in zip(parts, factors)])
    return pull, [peak, total]


def join_targets(parts):
    stats = [add([stats[i] for _, stats in parts]) for i in range(2)]
    return add([part for part, _ in parts]), stats


joins = {"pred": join_preds, "target": join_targets}


def send(info, place, pull, stats, outs, flipped):
    kept, *sent = outs
    share = pull.shape[1] // len(outs)
    high, tall = share + stat_rows, share + sent_rows
    flipped[...] = pull.T
    mine = pl.multiple_of(info[1] * share, share)
    kept[place * high : place * high + share, :] = flipped[pl.ds(mine, share), :]
    kept[place * high + share : (place + 1) * high, :] = padded(stats, pull.shape[0])
    terms = split_stats(stats)
    for s, out in enumerate(sent, 1):
        start = pl.multiple_of((info[1] ^ s) * share, share)
        out[place * tall : place * tall + share, :] = bare(flipped[pl.ds(start, share), :])
        out[place * tall + share : (place + 1) * tall, :] = terms


def whole(value):
    return pl.BlockSpec(value.shape, lambda *_: (0,) * len(value.shape))


def call(kernel, name, info, grid, ins, in_specs, outs, out_specs, scratch, flops, exps, room, passed=()):
    count, total = len(ins), len(ins) + len(outs)

    def without(*refs):
        return kernel(*refs[: 1 + total], *refs[1 + total + len(passed) :])

    outs = [*outs, *[jax.ShapeDtypeStruct(ins[i].shape, ins[i].dtype) for i in passed]]
    out_specs = [*out_specs, *[pl.BlockSpec(memory_space=pl.ANY)] * len(passed)]
    values = pl.pallas_call(
        without,
        grid_spec=pltpu.PrefetchScalarGridSpec(
            num_scalar_prefetch=1,
            grid=grid,
            in_specs=in_specs,
            out_specs=out_specs,
            scratch_shapes=scratch,
        ),
        out_shape=outs,
        input_output_aliases={1 + i: total - count + k for k, i in enumerate(passed)},
        compiler_params=pltpu.CompilerParams(vmem_limit_bytes=room * mebi),
        cost_estimate=pl.CostEstimate(flops=flops, bytes_accessed=flops // 128, transcendentals=exps),
        name=name,
    )(info, *ins)
    info, first = lax.optimization_barrier((info, values[0]))
    return info, first, *values[1:]


def placed_rows(info, quarters, block):
    part = quarters[0].shape[1]
    for s, quarter in enumerate(quarters):
        place = pl.multiple_of((info[1] ^ s) * part, part)
        block[pl.ds(place, part), :] = quarter[0]


def over_chunks(protos, width, step, unrolled=False):
    count = protos[0].shape[0] // width
    if unrolled:
        for i in range(count):
            for half, part in enumerate(protos):
                step(half * count + i, part[i * width : (i + 1) * width, :])
        return

    def both(i, carry):
        at = pl.ds(pl.multiple_of(i * width, width), width)
        for half, part in enumerate(protos):
            step(half * count + i, part[at, :])
        return carry

    lax.fori_loop(0, count, both, 0)


def column_sums(raw, peak):
    return jnp.sum(jnp.exp2((raw - peak) * code_scale), axis=0, keepdims=True)


def stats_kernel(fresh, info, *refs):
    if fresh:
        *codes, near, across, stats, copied = refs
        copied[...] = near[...]
    else:
        *codes, near, across, before, stats = refs
        stats[...] = before[...]
    protos, width = (near, across), stats.shape[2]

    def first(j, part):
        raw = scores(codes[0][...], part)
        peak = jnp.max(raw, axis=0, keepdims=True)
        stats[j, 0:1, :] = peak
        stats[j, 1:2, :] = column_sums(raw, peak)

    def kept_peak(rows, j, part):
        stats[j, 1:2, :] += column_sums(scores(rows, part), stats[j, 0:1, :])

    def new_peak(rows, j, part):
        raw = scores(rows, part)
        old, total = stats[j, 0:1, :], stats[j, 1:2, :]
        peak = jnp.maximum(old, jnp.max(raw, axis=0, keepdims=True))
        stats[j, 0:1, :] = peak
        stats[j, 1:2, :] = total * jnp.exp2((old - peak) * code_scale) + column_sums(raw, peak)

    def all_rows(add_rows, unrolled):
        for part in codes:
            rows = part[...].reshape(-1, part.shape[-1])
            over_chunks(protos, width, functools.partial(add_rows, rows), unrolled)

    if fresh:
        over_chunks(protos, width, first, True)
        return
    all_rows(kept_peak, True)
    worst = jnp.max(stats[:, 1:2, :])

    @pl.when(jnp.logical_not(worst < too_large))
    def _():
        stats[...] = before[...]
        all_rows(new_peak, False)


def stats_part(info, codes, protos, before):
    count, dim = protos[0].shape
    width = min(chunk, count)
    rows = sum(math.prod(part.shape[:-1]) for part in codes)
    outs = [jax.ShapeDtypeStruct((2 * count // width, stat_rows, width), jnp.float32)]
    ins, passed = [*codes, *protos], [len(codes), len(codes) + 1]
    if before is None:
        outs.append(jax.ShapeDtypeStruct(protos[0].shape, protos[0].dtype))
        passed = passed[1:]
    else:
        ins.append(before)
    return call(
        functools.partial(stats_kernel, before is None), "stats_part", info, (1,), ins,
        [whole(value) for value in ins], outs, [whole(out) for out in outs], [],
        4 * rows * count * dim, 2 * rows * count, 6, passed,
    )


def offset_kernel(info, stats, other, out):
    count = stats.shape[0] // 2
    for j in range(2 * count):
        here, there = stats[j], other[(j + count) % (2 * count)]
        peak = jnp.maximum(here[0:1], there[0:1])
        mass = here[1:2] * jnp.exp2((here[0:1] - peak) * code_scale) + there[1:2] * jnp.exp2(
            (there[0:1] - peak) * code_scale
        )
        offset = peak * code_scale + jnp.log2(mass)
        out[j] = jnp.broadcast_to(offset, out.shape[1:])


def offset_part(info, stats, other):
    return call(
        offset_kernel, "offset_part", info, (1,), [stats, other], [whole(stats)] * 2, [stats],
        [whole(stats)], [], 1 << 20, 0, 5,
    )


def weighted(value, protos):
    return jnp.dot(bare(value), protos, preferred_element_type=jnp.float32)


def row_of(combine, value):
    return combine(value.T, axis=0, keepdims=True)


def pred_logits(preds, protos, raws, top, j):
    raw = scores(preds[...], protos)
    raws[j] = raw
    top[...] = jnp.maximum(top[...], lane_fold(jnp.maximum, raw))


def pred_pull(protos, raws, top, total, pull, beside=None):
    width = raws.shape[2]
    stats = [row_of(jnp.max, top[...]) * pred_scale]
    peak = jnp.max(top[...], axis=1, keepdims=True)
    top[...] = jnp.broadcast_to(peak, top.shape)
    total[...] = jnp.zeros(total.shape, jnp.float32)
    pull[...] = jnp.zeros(pull.shape, jnp.float32)

    def step(j, protos):
        peak = jnp.concatenate([top[...]] * (width // 128), axis=1)
        value = jnp.exp2((raws[j] - peak) * pred_scale)
        total[...] += lane_fold(jnp.add, value)
        pull[...] += weighted(value, protos)
        if beside is not None:
            beside(j, protos)

    over_chunks(protos, width, step)
    return pull[...], [*stats, row_of(jnp.sum, total[...])]


def target_values(codes, protos, offset, total, j):
    value = jnp.exp2(scores(codes[...], protos) * code_scale - offset[j, 0:1, :])
    total[...] += lane_fold(jnp.add, value)
    return value


def target_step(codes, protos, offset, total, pull, j):
    pull[...] += weighted(target_values(codes, protos, offset, total, j), protos)


def target_stats(preds, total, pull):
    cross = lane_fold(jnp.add, pull[...] * preds[...].astype(jnp.float32))
    return [row_of(jnp.sum, total[...]), row_of(jnp.sum, cross)]


def pred_kernel(info, preds, near, across, *refs):
    *outs, raws, top, total, pull, flipped = refs
    protos = near, across
    top[...] = jnp.full(top.shape, low, jnp.float32)
    over_chunks(protos, raws.shape[2], lambda j, part: pred_logits(preds, part, raws, top, j))
    send(info, 0, *pred_pull(protos, raws, top, total, pull), outs, flipped)


def target_kernel(info, codes, preds, near, across, offset, *refs):
    *refs, total, pull, flipped = refs
    earlier, outs = refs[: len(refs) // 2], refs[len(refs) // 2 :]
    total[...] = jnp.zeros(total.shape, jnp.float32)
    pull[...] = jnp.zeros(pull.shape, jnp.float32)
    over_chunks(
        (near, across),
        offset.shape[2],
        lambda j, part: target_step(codes, part, offset, total, pull, j),
        True,
    )
    send(info, 0, pull[...], target_stats(preds, total, pull), outs, flipped)
    for part, out in zip(earlier, outs):
        out[part.shape[0] :, :] = part[...]


def both_kernel(proto_count, info, *refs):
    near, across, offset = refs[2 * proto_count : 2 * proto_count + 3]
    outs = refs[2 * proto_count + 3 : -10]
    raws, top, total, pull, flipped, codes, preds, held, pull_pred, total_pred = refs[-10:]
    protos = near, across
    placed_rows(info, refs[:proto_count], codes)
    placed_rows(info, refs[proto_count : 2 * proto_count], preds)
    top[...] = jnp.full(top.shape, low, jnp.float32)
    total[...] = jnp.zeros(total.shape, jnp.float32)
    pull[...] = jnp.zeros(pull.shape, jnp.float32)

    def step(j, part):
        pred_logits(preds, part, raws, top, j)
        held[j] = bare(target_values(codes, part, offset, total, j))

    def beside(j, part):
        pull[...] += jnp.dot(held[j], part, preferred_element_type=jnp.float32)

    over_chunks(protos, offset.shape[2], step)
    done = pred_pull(protos, raws, top, total_pred, pull_pred, beside)
    send(info, 0, pull[...], target_stats(preds, total, pull), outs, flipped)
    send(info, 1, *done, outs, flipped)


def rows_part(info, codes, preds, protos, offset, rows, proto_count, aways, earlier):
    count, dim = protos[0].shape
    share = dim // proto_count
    width, blocks = min(chunk, count), max(len(aways), 1)
    shapes = [(2 * count // width, rows, width), (rows, 128), (rows, 128), (rows, dim), (dim, rows)]
    scratch = [pltpu.VMEM(shape, jnp.float32) for shape in shapes]
    if codes is None:
        kernel, ins, passed = pred_kernel, [preds, *protos], (1, 2)
        specs = [whole(value) for value in ins]
    elif not aways:
        kernel, ins, passed = target_kernel, [codes, preds, *protos, offset, *earlier], ()
        specs, scratch = [whole(value) for value in ins], scratch[2:]
    else:
        kernel, ins = functools.partial(both_kernel, proto_count), [*codes, *preds, *protos, offset]
        passed = tuple(2 * proto_count + i for i in range(2))
        quarter = pl.BlockSpec((1, *codes[0].shape[1:]), lambda i, info: (aways[0] - 1 - i, 0, 0))
        specs = [quarter] * (2 * proto_count) + [whole(value) for value in ins[-3:]]
        scratch = [*scratch] + [pltpu.VMEM((rows, dim), jnp.bfloat16)] * 2
        scratch += [pltpu.VMEM(shapes[0], jnp.bfloat16)]
        scratch += [pltpu.VMEM(shape, jnp.float32) for shape in ((rows, dim), (rows, 128))]
    parts, work = 2 if codes is not None else 1, 2 * blocks if aways else 1
    high, tall = parts * (share + stat_rows), parts * (share + sent_rows)
    outs = [jax.ShapeDtypeStruct((high, blocks * rows), jnp.float32)]
    outs += [jax.ShapeDtypeStruct((tall, blocks * rows), jnp.bfloat16)] * (proto_count - 1)
    return call(
        kernel, "rows_part", info, (blocks,), ins, specs, outs,
        [pl.BlockSpec((out.shape[0], rows), lambda i, info: (0, i)) for out in outs], scratch,
        work * 8 * rows * count * dim, work * 2 * rows * count,
        6 if kernel is target_kernel else 20, passed,
    )


names = ["target", "pred"]


def packed_far(target, pred):
    pull, stats = pred
    high = bare(pull)
    rest = bare(pull - high.astype(jnp.float32))
    return jnp.concatenate([bare(target[0]), high, rest, split_stats([*target[1], *stats])], axis=0)


def parted_far(value):
    share = (value.shape[0] - sent_rows) // 3
    target, high, rest = [
        value[i * share : (i + 1) * share, :].astype(jnp.float32) for i in range(3)
    ]
    stats = join_stats(value[3 * share :, :], 4)
    return {"target": (target, stats[:2]), "pred": (high + rest, stats[2:])}


def joined(parts, at=slice(None), others=()):
    kept, *sent = parts
    high, tall = kept.shape[0] // len(names), sent[0].shape[0] // len(names)
    return [
        joins[name](
            [parted(kept[i * high : (i + 1) * high, at])]
            + [parted_sent(part[i * tall : (i + 1) * tall, at]) for part in sent]
            + [part[name] for part in others]
        )
        for i, name in enumerate(names)
    ]


def spread_kernel(count, info, *refs):
    parts, outs = refs[:count], refs[count:]
    rows = outs[0].shape[1]
    for block, out in enumerate(outs):
        out[...] = packed_far(*joined(parts, slice(block * rows, (block + 1) * rows)))


def join_spread(info, parts, rows):
    high, length = parts[0].shape
    share = high // len(names) - stat_rows
    outs = [
        jax.ShapeDtypeStruct((3 * share + sent_rows, rows), jnp.bfloat16)
        for _ in range(length // rows)
    ]
    return call(
        functools.partial(spread_kernel, len(parts)), "join_spread", info, (1,), parts,
        [whole(part) for part in parts], outs, [whole(out) for out in outs], [], 1 << 20, 0, 5,
    )


def final_kernel(count, info, *refs):
    parts, far, (loss, pull) = refs[:count], refs[count:-2], refs[-2:]
    far = [parted_far(part[...]) for part in far]
    (target, (mass, cross)), (pred, (peak, total)) = joined(parts, others=far)
    pull[...] = target / mass - pred / total
    loss[...] = peak * log2 + jnp.log(total) - cross / mass / pred_temp


def finish(info, own, others):
    high, length = own[0].shape
    outs = [
        jax.ShapeDtypeStruct((1, length), jnp.float32),
        jax.ShapeDtypeStruct((high // len(names) - stat_rows, length), jnp.float32),
    ]
    ins = [*own, *others]
    return call(
        functools.partial(final_kernel, len(own)), "finish", info, (1,), ins,
        [whole(value) for value in ins], outs, [whole(out) for out in outs], [], 1 << 20, 0, 5,
    )[1:]


def swap(value, axis, bits):
    count = lax.axis_size(axis)
    return lax.ppermute(value, axis, [(i, i ^ bits) for i in range(count)])


def body(codes_view, pred_view, prototypes):
    rows = codes_view.shape[0]
    dp_count, proto_count = lax.axis_size("dp"), lax.axis_size("proto")
    z_count = dp_count // 2
    me, proto = lax.axis_index("dp"), lax.axis_index("proto")
    info = jnp.stack([me // 2, proto]).astype(jnp.int32)

    def sent(values):
        return [values[0]] + [swap(value, "proto", s) for s, value in enumerate(values[1:], 1)]

    protos = prototypes, swap(prototypes, "dp", 1)
    part = rows // proto_count
    piece = jnp.concatenate(
        [
            lax.dynamic_slice_in_dim(view, proto * part, part, 0)
            for view in (codes_view, pred_view)
        ]
    )
    quarters = [swap(piece, "dp", 2 * t) for t in range(1, z_count)]

    def around(value):
        return [value] + [swap(value, "proto", s) for s in range(1, proto_count)]

    info, stats, *protos = stats_part(info, [codes_view], protos, None)
    info, *values = rows_part(info, None, pred_view, protos, None, rows, proto_count, (), None)
    *earlier, near, across = values
    quarters, info = lax.optimization_barrier((quarters, info))
    codes = around(jnp.stack([value[:part] for value in quarters]))
    preds = jnp.stack([value[part:] for value in quarters])
    info, stats, *protos = stats_part(info, codes[:1], (near, across), stats)
    preds, info = lax.optimization_barrier((preds, info))
    preds = around(preds)
    info, stats, *protos = stats_part(info, codes[1:], protos, stats)
    info, offset = offset_part(info, stats, swap(stats, "dp", 1))

    def far_rows(info, protos, aways):
        info, *out, near, across = rows_part(
            info, codes, preds, protos, offset, rows, proto_count, aways, None
        )
        return info, sent(out), (near, across)

    aways = range(z_count - 1, 1, -1)
    info, far, protos = far_rows(info, protos, aways)
    info, late, protos = far_rows(info, protos, range(1, 0, -1))
    info, *far = join_spread(info, far, rows)
    far = [swap(part, "dp", 2 * away) for away, part in zip(aways, far)]
    info, *out = rows_part(
        info, codes_view, pred_view, protos, offset, rows, proto_count, (), earlier
    )
    own = sent(out)
    far, late = lax.optimization_barrier((far, late))
    info, part = join_spread(info, late, rows)
    loss, pull = finish(info, own, [*far, swap(part, "dp", 2)])
    return (loss.reshape(rows), pull.T)


def solution(mesh):
    placed = (P("dp", None), P("dp", None), P(("proto", "dp"), None))
    return jax.shard_map(
        body, mesh=mesh, in_specs=placed, out_specs=(P("dp"), P("dp", "proto")), check_vma=False
    )
```

```python
import functools
import math

import jax
import jax.numpy as jnp
from jax import lax
from jax.experimental import pallas as pl
from jax.experimental.pallas import tpu as pltpu
from jax.sharding import PartitionSpec as P

code_temp = 0.05
pred_temp = 0.1
code_scale = math.log2(math.e) / code_temp
pred_scale = math.log2(math.e) / pred_temp
log2 = math.log(2.0)
too_large = 2.0**100
stat_rows = 8
sent_rows = 16
low = -1e30
chunk = 1024
mebi = 1024 * 1024


def scores(embeds, protos):
    return lax.dot_general(
        embeds, protos, (((1,), (1,)), ((), ())), preferred_element_type=jnp.float32
    )


def bare(value):
    return value.astype(jnp.bfloat16)


def add(parts):
    return functools.reduce(jnp.add, parts)


def lane_fold(combine, value):
    parts = [value[:, i : i + 128] for i in range(0, value.shape[1], 128)]
    return functools.reduce(combine, parts)


def padded(rows, width):
    filler = jnp.zeros((stat_rows - len(rows), width), jnp.float32)
    return jnp.concatenate([*rows, filler], axis=0)


def split_stats(stats):
    terms = []
    for row in stats:
        for _ in range(3):
            term = bare(row)
            row = row - term.astype(jnp.float32)
            terms.append(term)
    filler = jnp.zeros((sent_rows - len(terms), stats[0].shape[1]), jnp.bfloat16)
    return jnp.concatenate([*terms, filler], axis=0)


def join_stats(terms, count):
    wide = terms.astype(jnp.float32)
    return [add([wide[3 * i + j : 3 * i + j + 1] for j in range(3)]) for i in range(count)]


def parted(value):
    share = value.shape[0] - stat_rows
    return value[:share, :], [value[share + i : share + i + 1, :] for i in range(2)]


def parted_sent(value):
    share = value.shape[0] - sent_rows
    return value[:share, :].astype(jnp.float32), join_stats(value[share:, :], 2)


def packed(part):
    pull, stats = part
    return jnp.concatenate([pull, padded(stats, pull.shape[1])], axis=0)


def join_preds(parts):
    peak = functools.reduce(jnp.maximum, [stats[0] for _, stats in parts])
    factors = [jnp.exp2(stats[0] - peak) for _, stats in parts]
    pull = add([part * factor for (part, _), factor in zip(parts, factors)])
    total = add([stats[1] * factor for (_, stats), factor in zip(parts, factors)])
    return pull, [peak, total]


def join_targets(parts):
    stats = [add([stats[i] for _, stats in parts]) for i in range(2)]
    return add([part for part, _ in parts]), stats


joins = {"pred": join_preds, "target": join_targets}


def send(info, place, pull, stats, outs, flipped):
    kept, *sent = outs
    share = pull.shape[1] // len(outs)
    high, tall = share + stat_rows, share + sent_rows
    flipped[...] = pull.T
    mine = pl.multiple_of(info[1] * share, share)
    kept[place * high : place * high + share, :] = flipped[pl.ds(mine, share), :]
    kept[place * high + share : (place + 1) * high, :] = padded(stats, pull.shape[0])
    terms = split_stats(stats)
    for s, out in enumerate(sent, 1):
        start = pl.multiple_of((info[1] ^ s) * share, share)
        out[place * tall : place * tall + share, :] = bare(flipped[pl.ds(start, share), :])
        out[place * tall + share : (place + 1) * tall, :] = terms


def whole(value):
    return pl.BlockSpec(value.shape, lambda *_: (0,) * len(value.shape))


def call(kernel, name, info, grid, ins, in_specs, outs, out_specs, scratch, flops, exps, room, passed=()):
    count, total = len(ins), len(ins) + len(outs)

    def without(*refs):
        return kernel(*refs[: 1 + total], *refs[1 + total + len(passed) :])

    outs = [*outs, *[jax.ShapeDtypeStruct(ins[i].shape, ins[i].dtype) for i in passed]]
    out_specs = [*out_specs, *[pl.BlockSpec(memory_space=pl.ANY)] * len(passed)]
    values = pl.pallas_call(
        without,
        grid_spec=pltpu.PrefetchScalarGridSpec(
            num_scalar_prefetch=1,
            grid=grid,
            in_specs=in_specs,
            out_specs=out_specs,
            scratch_shapes=scratch,
        ),
        out_shape=outs,
        input_output_aliases={1 + i: total - count + k for k, i in enumerate(passed)},
        compiler_params=pltpu.CompilerParams(vmem_limit_bytes=room * mebi),
        cost_estimate=pl.CostEstimate(flops=flops, bytes_accessed=flops // 128, transcendentals=exps),
        name=name,
    )(info, *ins)
    info, first = lax.optimization_barrier((info, values[0]))
    return info, first, *values[1:]


def placed_rows(info, quarters, block):
    part = quarters[0].shape[1]
    for s, quarter in enumerate(quarters):
        place = pl.multiple_of((info[1] ^ s) * part, part)
        block[pl.ds(place, part), :] = quarter[0]


def over_chunks(protos, width, step, unrolled=False):
    count = protos[0].shape[0] // width
    if unrolled:
        for i in range(count):
            for half, part in enumerate(protos):
                step(half * count + i, part[i * width : (i + 1) * width, :])
        return

    def both(i, carry):
        at = pl.ds(pl.multiple_of(i * width, width), width)
        for half, part in enumerate(protos):
            step(half * count + i, part[at, :])
        return carry

    lax.fori_loop(0, count, both, 0)


def column_sums(raw, peak):
    return jnp.sum(jnp.exp2((raw - peak) * code_scale), axis=0, keepdims=True)


def stats_kernel(fresh, info, *refs):
    if fresh:
        *codes, near, across, stats, copied = refs
        copied[...] = near[...]
    else:
        *codes, near, across, before, stats = refs
        stats[...] = before[...]
    protos, width = (near, across), stats.shape[2]

    def first(j, part):
        raw = scores(codes[0][...], part)
        peak = jnp.max(raw, axis=0, keepdims=True)
        stats[j, 0:1, :] = peak
        stats[j, 1:2, :] = column_sums(raw, peak)

    def kept_peak(rows, j, part):
        stats[j, 1:2, :] += column_sums(scores(rows, part), stats[j, 0:1, :])

    def new_peak(rows, j, part):
        raw = scores(rows, part)
        old, total = stats[j, 0:1, :], stats[j, 1:2, :]
        peak = jnp.maximum(old, jnp.max(raw, axis=0, keepdims=True))
        stats[j, 0:1, :] = peak
        stats[j, 1:2, :] = total * jnp.exp2((old - peak) * code_scale) + column_sums(raw, peak)

    def all_rows(add_rows, unrolled):
        for part in codes:
            rows = part[...].reshape(-1, part.shape[-1])
            over_chunks(protos, width, functools.partial(add_rows, rows), unrolled)

    if fresh:
        over_chunks(protos, width, first, True)
        return
    all_rows(kept_peak, True)
    worst = jnp.max(stats[:, 1:2, :])

    @pl.when(jnp.logical_not(worst < too_large))
    def _():
        stats[...] = before[...]
        all_rows(new_peak, False)


def stats_part(info, codes, protos, before):
    count, dim = protos[0].shape
    width = min(chunk, count)
    rows = sum(math.prod(part.shape[:-1]) for part in codes)
    outs = [jax.ShapeDtypeStruct((2 * count // width, stat_rows, width), jnp.float32)]
    ins, passed = [*codes, *protos], [len(codes), len(codes) + 1]
    if before is None:
        outs.append(jax.ShapeDtypeStruct(protos[0].shape, protos[0].dtype))
        passed = passed[1:]
    else:
        ins.append(before)
    return call(
        functools.partial(stats_kernel, before is None), "stats_part", info, (1,), ins,
        [whole(value) for value in ins], outs, [whole(out) for out in outs], [],
        4 * rows * count * dim, 2 * rows * count, 12, passed,
    )


def offset_kernel(info, stats, other, out):
    count = stats.shape[0] // 2
    for j in range(2 * count):
        here, there = stats[j], other[(j + count) % (2 * count)]
        peak = jnp.maximum(here[0:1], there[0:1])
        mass = here[1:2] * jnp.exp2((here[0:1] - peak) * code_scale) + there[1:2] * jnp.exp2(
            (there[0:1] - peak) * code_scale
        )
        offset = peak * code_scale + jnp.log2(mass)
        out[j] = jnp.broadcast_to(offset, out.shape[1:])


def offset_part(info, stats, other):
    return call(
        offset_kernel, "offset_part", info, (1,), [stats, other], [whole(stats)] * 2, [stats],
        [whole(stats)], [], 1 << 20, 0, 5,
    )


def weighted(value, protos):
    return jnp.dot(bare(value), protos, preferred_element_type=jnp.float32)


def row_of(combine, value):
    return combine(value.T, axis=0, keepdims=True)


def pred_logits(preds, protos, raws, top, j):
    raw = scores(preds[...], protos)
    raws[j] = raw
    top[...] = jnp.maximum(top[...], lane_fold(jnp.maximum, raw))


def pred_pull(protos, raws, top, total, pull, beside=None):
    width = raws.shape[2]
    stats = [row_of(jnp.max, top[...]) * pred_scale]
    peak = jnp.max(top[...], axis=1, keepdims=True)
    top[...] = jnp.broadcast_to(peak, top.shape)
    total[...] = jnp.zeros(total.shape, jnp.float32)
    pull[...] = jnp.zeros(pull.shape, jnp.float32)

    def step(j, protos):
        peak = jnp.concatenate([top[...]] * (width // 128), axis=1)
        value = jnp.exp2((raws[j] - peak) * pred_scale)
        total[...] += lane_fold(jnp.add, value)
        pull[...] += weighted(value, protos)
        if beside is not None:
            beside(j, protos)

    over_chunks(protos, width, step)
    return pull[...], [*stats, row_of(jnp.sum, total[...])]


def target_values(codes, protos, offset, total, j):
    value = jnp.exp2(scores(codes[...], protos) * code_scale - offset[j, 0:1, :])
    total[...] += lane_fold(jnp.add, value)
    return value


def target_step(codes, protos, offset, total, pull, j):
    pull[...] += weighted(target_values(codes, protos, offset, total, j), protos)


def target_stats(preds, total, pull):
    cross = lane_fold(jnp.add, pull[...] * preds[...].astype(jnp.float32))
    return [row_of(jnp.sum, total[...]), row_of(jnp.sum, cross)]


def pred_kernel(info, preds, near, across, *refs):
    *outs, raws, top, total, pull, flipped = refs
    protos = near, across
    top[...] = jnp.full(top.shape, low, jnp.float32)
    over_chunks(protos, raws.shape[2], lambda j, part: pred_logits(preds, part, raws, top, j))
    send(info, 0, *pred_pull(protos, raws, top, total, pull), outs, flipped)


def target_kernel(info, codes, preds, near, across, offset, *refs):
    *refs, total, pull, flipped = refs
    earlier, outs = refs[: len(refs) // 2], refs[len(refs) // 2 :]
    total[...] = jnp.zeros(total.shape, jnp.float32)
    pull[...] = jnp.zeros(pull.shape, jnp.float32)
    over_chunks(
        (near, across),
        offset.shape[2],
        lambda j, part: target_step(codes, part, offset, total, pull, j),
        True,
    )
    send(info, 0, pull[...], target_stats(preds, total, pull), outs, flipped)
    for part, out in zip(earlier, outs):
        out[part.shape[0] :, :] = part[...]


def both_kernel(proto_count, info, *refs):
    near, across, offset = refs[2 * proto_count : 2 * proto_count + 3]
    outs = refs[2 * proto_count + 3 : -10]
    raws, top, total, pull, flipped, codes, preds, held, pull_pred, total_pred = refs[-10:]
    protos = near, across
    placed_rows(info, refs[:proto_count], codes)
    placed_rows(info, refs[proto_count : 2 * proto_count], preds)
    top[...] = jnp.full(top.shape, low, jnp.float32)
    total[...] = jnp.zeros(total.shape, jnp.float32)
    pull[...] = jnp.zeros(pull.shape, jnp.float32)

    def step(j, part):
        pred_logits(preds, part, raws, top, j)
        held[j] = bare(target_values(codes, part, offset, total, j))

    def beside(j, part):
        pull[...] += jnp.dot(held[j], part, preferred_element_type=jnp.float32)

    over_chunks(protos, offset.shape[2], step)
    done = pred_pull(protos, raws, top, total_pred, pull_pred, beside)
    send(info, 0, pull[...], target_stats(preds, total, pull), outs, flipped)
    send(info, 1, *done, outs, flipped)


def rows_part(info, codes, preds, protos, offset, rows, proto_count, away, earlier):
    count, dim = protos[0].shape
    share = dim // proto_count
    width = min(chunk, count)
    shapes = [(2 * count // width, rows, width), (rows, 128), (rows, 128), (rows, dim), (dim, rows)]
    scratch = [pltpu.VMEM(shape, jnp.float32) for shape in shapes]
    if codes is None:
        kernel, ins, passed = pred_kernel, [preds, *protos], (1, 2)
        specs = [whole(value) for value in ins]
    elif not away:
        kernel, ins, passed = target_kernel, [codes, preds, *protos, offset, *earlier], ()
        specs, scratch = [whole(value) for value in ins], scratch[2:]
    else:
        kernel, ins = functools.partial(both_kernel, proto_count), [*codes, *preds, *protos, offset]
        passed = tuple(2 * proto_count + i for i in range(2))
        quarter = pl.BlockSpec((1, *codes[0].shape[1:]), lambda i, info: (away - 1, 0, 0))
        specs = [quarter] * (2 * proto_count) + [whole(value) for value in ins[-3:]]
        scratch = [*scratch] + [pltpu.VMEM((rows, dim), jnp.bfloat16)] * 2
        scratch += [pltpu.VMEM(shapes[0], jnp.bfloat16)]
        scratch += [pltpu.VMEM(shape, jnp.float32) for shape in ((rows, dim), (rows, 128))]
    parts, work = 2 if codes is not None else 1, 2 if away else 1
    high, tall = parts * (share + stat_rows), parts * (share + sent_rows)
    outs = [jax.ShapeDtypeStruct((high, rows), jnp.float32)]
    outs += [jax.ShapeDtypeStruct((tall, rows), jnp.bfloat16)] * (proto_count - 1)
    return call(
        kernel, "rows_part", info, (1,), ins, specs, outs, [whole(out) for out in outs], scratch,
        work * 8 * rows * count * dim, work * 2 * rows * count,
        12 if kernel is target_kernel else 26, passed,
    )


names = ["target", "pred"]


def packed_far(target, pred):
    pull, stats = pred
    high = bare(pull)
    rest = bare(pull - high.astype(jnp.float32))
    return jnp.concatenate([bare(target[0]), high, rest, split_stats([*target[1], *stats])], axis=0)


def parted_far(value):
    share = (value.shape[0] - sent_rows) // 3
    target, high, rest = [
        value[i * share : (i + 1) * share, :].astype(jnp.float32) for i in range(3)
    ]
    stats = join_stats(value[3 * share :, :], 4)
    return {"target": (target, stats[:2]), "pred": (high + rest, stats[2:])}


def joined(parts, others=()):
    kept, *sent = parts
    high, tall = kept.shape[0] // len(names), sent[0].shape[0] // len(names)
    return [
        joins[name](
            [parted(kept[i * high : (i + 1) * high, :])]
            + [parted_sent(part[i * tall : (i + 1) * tall, :]) for part in sent]
            + [part[name] for part in others]
        )
        for i, name in enumerate(names)
    ]


def spread_kernel(info, *refs):
    *parts, out = refs
    out[...] = packed_far(*joined(parts))


def join_spread(info, parts):
    high, rows = parts[0].shape
    share = high // len(names) - stat_rows
    out = jax.ShapeDtypeStruct((3 * share + sent_rows, rows), jnp.bfloat16)
    return call(
        spread_kernel, "join_spread", info, (1,), parts, [whole(part) for part in parts], [out],
        [whole(out)], [], 1 << 20, 0, 5,
    )


def final_kernel(count, info, *refs):
    parts, far, (loss, pull) = refs[:count], refs[count:-2], refs[-2:]
    far = [parted_far(part[...]) for part in far]
    (target, (mass, cross)), (pred, (peak, total)) = joined(parts, far)
    pull[...] = target / mass - pred / total
    loss[...] = peak * log2 + jnp.log(total) - cross / mass / pred_temp


def finish(info, own, others):
    high, length = own[0].shape
    outs = [
        jax.ShapeDtypeStruct((1, length), jnp.float32),
        jax.ShapeDtypeStruct((high // len(names) - stat_rows, length), jnp.float32),
    ]
    ins = [*own, *others]
    return call(
        functools.partial(final_kernel, len(own)), "finish", info, (1,), ins,
        [whole(value) for value in ins], outs, [whole(out) for out in outs], [], 1 << 20, 0, 5,
    )[1:]


def swap(value, axis, bits):
    count = lax.axis_size(axis)
    return lax.ppermute(value, axis, [(i, i ^ bits) for i in range(count)])


def body(codes_view, pred_view, prototypes):
    rows = codes_view.shape[0]
    dp_count, proto_count = lax.axis_size("dp"), lax.axis_size("proto")
    z_count = dp_count // 2
    me, proto = lax.axis_index("dp"), lax.axis_index("proto")
    info = jnp.stack([me // 2, proto]).astype(jnp.int32)

    def sent(values):
        return [values[0]] + [swap(value, "proto", s) for s, value in enumerate(values[1:], 1)]

    protos = prototypes, swap(prototypes, "dp", 1)
    part = rows // proto_count
    piece = jnp.concatenate(
        [
            lax.dynamic_slice_in_dim(view, proto * part, part, 0)
            for view in (codes_view, pred_view)
        ]
    )
    quarters = [swap(piece, "dp", 2 * t) for t in range(1, z_count)]

    def around(value):
        return [value] + [swap(value, "proto", s) for s in range(1, proto_count)]

    info, stats, *protos = stats_part(info, [codes_view], protos, None)
    info, *values = rows_part(info, None, pred_view, protos, None, rows, proto_count, 0, None)
    *earlier, near, across = values
    quarters, info = lax.optimization_barrier((quarters, info))
    codes = around(jnp.stack([value[:part] for value in quarters]))
    preds = jnp.stack([value[part:] for value in quarters])
    info, stats, *protos = stats_part(info, codes[:1], (near, across), stats)
    preds, info = lax.optimization_barrier((preds, info))
    preds = around(preds)
    info, stats, *protos = stats_part(info, codes[1:], protos, stats)
    info, offset = offset_part(info, stats, swap(stats, "dp", 1))

    far, waiting = [], []
    for away in range(z_count - 1, 0, -1):
        info, *values = rows_part(
            info, codes, preds, protos, offset, rows, proto_count, away, None
        )
        *out, near, across = values
        protos = near, across
        out = sent(out)
        for past, arrived in waiting:
            if far:
                far, arrived = lax.optimization_barrier((far, arrived))
            info, part = join_spread(info, arrived)
            far.append(swap(part, "dp", 2 * past))
        waiting = [(away, out)]
    info, *out = rows_part(
        info, codes_view, pred_view, protos, offset, rows, proto_count, 0, earlier
    )
    own = sent(out)
    ((past, arrived),) = waiting
    far, arrived = lax.optimization_barrier((far, arrived))
    info, part = join_spread(info, arrived)
    own[1], part = lax.optimization_barrier((own[1], part))
    loss, pull = finish(info, own, [*far, swap(part, "dp", 2 * past)])
    return (loss.reshape(rows), pull.T)


def solution(mesh):
    placed = (P("dp", None), P("dp", None), P(("proto", "dp"), None))
    return jax.shard_map(
        body, mesh=mesh, in_specs=placed, out_specs=(P("dp"), P("dp", "proto")), check_vma=False
    )
```

```python
import functools
import math

import jax
import jax.numpy as jnp
from jax import lax
from jax.experimental import pallas as pl
from jax.experimental.pallas import tpu as pltpu
from jax.sharding import PartitionSpec as P

code_temp = 0.05
pred_temp = 0.1
code_scale = math.log2(math.e) / code_temp
pred_scale = math.log2(math.e) / pred_temp
log2 = math.log(2.0)
too_large = 2.0**100
stat_rows = 8
sent_rows = 16
low = -1e30
chunk = 2048
mebi = 1024 * 1024


def scores(embeds, protos):
    return lax.dot_general(
        embeds, protos, (((1,), (1,)), ((), ())), preferred_element_type=jnp.float32
    )


def bare(value):
    return value.astype(jnp.bfloat16)


def add(parts):
    return functools.reduce(jnp.add, parts)


def lane_fold(combine, value):
    parts = [value[:, i : i + 128] for i in range(0, value.shape[1], 128)]
    return functools.reduce(combine, parts)


def padded(rows, width):
    filler = jnp.zeros((stat_rows - len(rows), width), jnp.float32)
    return jnp.concatenate([*rows, filler], axis=0)


def split_stats(stats):
    terms = []
    for row in stats:
        for _ in range(3):
            term = bare(row)
            row = row - term.astype(jnp.float32)
            terms.append(term)
    filler = jnp.zeros((sent_rows - len(terms), stats[0].shape[1]), jnp.bfloat16)
    return jnp.concatenate([*terms, filler], axis=0)


def join_stats(terms, count):
    wide = terms.astype(jnp.float32)
    return [add([wide[3 * i + j : 3 * i + j + 1] for j in range(3)]) for i in range(count)]


def parted(value):
    share = value.shape[0] - stat_rows
    return value[:share, :], [value[share + i : share + i + 1, :] for i in range(2)]


def parted_sent(value):
    share = value.shape[0] - sent_rows
    return value[:share, :].astype(jnp.float32), join_stats(value[share:, :], 2)


def packed(part):
    pull, stats = part
    return jnp.concatenate([pull, padded(stats, pull.shape[1])], axis=0)


def join_preds(parts):
    peak = functools.reduce(jnp.maximum, [stats[0] for _, stats in parts])
    factors = [jnp.exp2(stats[0] - peak) for _, stats in parts]
    pull = add([part * factor for (part, _), factor in zip(parts, factors)])
    total = add([stats[1] * factor for (_, stats), factor in zip(parts, factors)])
    return pull, [peak, total]


def join_targets(parts):
    stats = [add([stats[i] for _, stats in parts]) for i in range(2)]
    return add([part for part, _ in parts]), stats


joins = {"pred": join_preds, "target": join_targets}


def send(info, place, pull, stats, outs, flipped):
    kept, *sent = outs
    share = pull.shape[1] // len(outs)
    high, tall = share + stat_rows, share + sent_rows
    flipped[...] = pull.T
    mine = pl.multiple_of(info[1] * share, share)
    kept[place * high : place * high + share, :] = flipped[pl.ds(mine, share), :]
    kept[place * high + share : (place + 1) * high, :] = padded(stats, pull.shape[0])
    terms = split_stats(stats)
    for s, out in enumerate(sent, 1):
        start = pl.multiple_of((info[1] ^ s) * share, share)
        out[place * tall : place * tall + share, :] = bare(flipped[pl.ds(start, share), :])
        out[place * tall + share : (place + 1) * tall, :] = terms


def whole(value):
    return pl.BlockSpec(value.shape, lambda *_: (0,) * len(value.shape))


def call(kernel, name, info, grid, ins, in_specs, outs, out_specs, scratch, flops, exps, room, passed=()):
    count, total = len(ins), len(ins) + len(outs)

    def without(*refs):
        return kernel(*refs[: 1 + total], *refs[1 + total + len(passed) :])

    outs = [*outs, *[jax.ShapeDtypeStruct(ins[i].shape, ins[i].dtype) for i in passed]]
    out_specs = [*out_specs, *[pl.BlockSpec(memory_space=pl.ANY)] * len(passed)]
    values = pl.pallas_call(
        without,
        grid_spec=pltpu.PrefetchScalarGridSpec(
            num_scalar_prefetch=1,
            grid=grid,
            in_specs=in_specs,
            out_specs=out_specs,
            scratch_shapes=scratch,
        ),
        out_shape=outs,
        input_output_aliases={1 + i: total - count + k for k, i in enumerate(passed)},
        compiler_params=pltpu.CompilerParams(vmem_limit_bytes=room * mebi),
        cost_estimate=pl.CostEstimate(flops=flops, bytes_accessed=flops // 128, transcendentals=exps),
        name=name,
    )(info, *ins)
    info, first = lax.optimization_barrier((info, values[0]))
    return info, first, *values[1:]


def placed_rows(info, quarters, block):
    part = quarters[0].shape[1]
    for s, quarter in enumerate(quarters):
        place = pl.multiple_of((info[1] ^ s) * part, part)
        block[pl.ds(place, part), :] = quarter[0]


def over_chunks(protos, width, step, unrolled=False):
    count = protos[0].shape[0] // width
    if unrolled:
        for i in range(count):
            for half, part in enumerate(protos):
                step(half * count + i, part[i * width : (i + 1) * width, :])
        return

    def both(i, carry):
        at = pl.ds(pl.multiple_of(i * width, width), width)
        for half, part in enumerate(protos):
            step(half * count + i, part[at, :])
        return carry

    lax.fori_loop(0, count, both, 0)


def column_sums(raw, peak):
    return jnp.sum(jnp.exp2((raw - peak) * code_scale), axis=0, keepdims=True)


def stats_kernel(fresh, info, *refs):
    if fresh:
        *codes, near, across, stats, copied = refs
        copied[...] = near[...]
    else:
        *codes, near, across, before, stats = refs
        stats[...] = before[...]
    protos, width = (near, across), stats.shape[2]

    def first(j, part):
        raw = scores(codes[0][...], part)
        peak = jnp.max(raw, axis=0, keepdims=True)
        stats[j, 0:1, :] = peak
        stats[j, 1:2, :] = column_sums(raw, peak)

    def kept_peak(rows, j, part):
        stats[j, 1:2, :] += column_sums(scores(rows, part), stats[j, 0:1, :])

    def new_peak(rows, j, part):
        raw = scores(rows, part)
        old, total = stats[j, 0:1, :], stats[j, 1:2, :]
        peak = jnp.maximum(old, jnp.max(raw, axis=0, keepdims=True))
        stats[j, 0:1, :] = peak
        stats[j, 1:2, :] = total * jnp.exp2((old - peak) * code_scale) + column_sums(raw, peak)

    def all_rows(add_rows, unrolled):
        for part in codes:
            rows = part[...].reshape(-1, part.shape[-1])
            over_chunks(protos, width, functools.partial(add_rows, rows), unrolled)

    if fresh:
        over_chunks(protos, width, first, True)
        return
    all_rows(kept_peak, True)
    worst = jnp.max(stats[:, 1:2, :])

    @pl.when(jnp.logical_not(worst < too_large))
    def _():
        stats[...] = before[...]
        all_rows(new_peak, False)


def stats_part(info, codes, protos, before):
    count, dim = protos[0].shape
    width = min(chunk, count)
    rows = sum(math.prod(part.shape[:-1]) for part in codes)
    outs = [jax.ShapeDtypeStruct((2 * count // width, stat_rows, width), jnp.float32)]
    ins, passed = [*codes, *protos], [len(codes), len(codes) + 1]
    if before is None:
        outs.append(jax.ShapeDtypeStruct(protos[0].shape, protos[0].dtype))
        passed = passed[1:]
    else:
        ins.append(before)
    return call(
        functools.partial(stats_kernel, before is None), "stats_part", info, (1,), ins,
        [whole(value) for value in ins], outs, [whole(out) for out in outs], [],
        4 * rows * count * dim, 2 * rows * count, 20, passed,
    )


def offset_kernel(info, stats, other, out):
    count = stats.shape[0] // 2
    for j in range(2 * count):
        here, there = stats[j], other[(j + count) % (2 * count)]
        peak = jnp.maximum(here[0:1], there[0:1])
        mass = here[1:2] * jnp.exp2((here[0:1] - peak) * code_scale) + there[1:2] * jnp.exp2(
            (there[0:1] - peak) * code_scale
        )
        offset = peak * code_scale + jnp.log2(mass)
        out[j] = jnp.broadcast_to(offset, out.shape[1:])


def offset_part(info, stats, other):
    return call(
        offset_kernel, "offset_part", info, (1,), [stats, other], [whole(stats)] * 2, [stats],
        [whole(stats)], [], 1 << 20, 0, 5,
    )


def weighted(value, protos):
    return jnp.dot(bare(value), protos, preferred_element_type=jnp.float32)


def row_of(combine, value):
    return combine(value.T, axis=0, keepdims=True)


def pred_logits(preds, protos, raws, top, j):
    raw = scores(preds[...], protos)
    raws[j] = raw
    top[...] = jnp.maximum(top[...], lane_fold(jnp.maximum, raw))


def pred_pull(protos, raws, top, total, pull, beside=None):
    width = raws.shape[2]
    stats = [row_of(jnp.max, top[...]) * pred_scale]
    peak = jnp.max(top[...], axis=1, keepdims=True)
    top[...] = jnp.broadcast_to(peak, top.shape)
    total[...] = jnp.zeros(total.shape, jnp.float32)
    pull[...] = jnp.zeros(pull.shape, jnp.float32)

    def step(j, protos):
        peak = jnp.concatenate([top[...]] * (width // 128), axis=1)
        value = jnp.exp2((raws[j] - peak) * pred_scale)
        total[...] += lane_fold(jnp.add, value)
        pull[...] += weighted(value, protos)
        if beside is not None:
            beside(j, protos)

    over_chunks(protos, width, step)
    return pull[...], [*stats, row_of(jnp.sum, total[...])]


def target_values(codes, protos, offset, total, j):
    value = jnp.exp2(scores(codes[...], protos) * code_scale - offset[j, 0:1, :])
    total[...] += lane_fold(jnp.add, value)
    return value


def target_step(codes, protos, offset, total, pull, j):
    pull[...] += weighted(target_values(codes, protos, offset, total, j), protos)


def target_stats(preds, total, pull):
    cross = lane_fold(jnp.add, pull[...] * preds[...].astype(jnp.float32))
    return [row_of(jnp.sum, total[...]), row_of(jnp.sum, cross)]


def pred_kernel(info, preds, near, across, *refs):
    *outs, raws, top, total, pull, flipped = refs
    protos = near, across
    top[...] = jnp.full(top.shape, low, jnp.float32)
    over_chunks(protos, raws.shape[2], lambda j, part: pred_logits(preds, part, raws, top, j))
    send(info, 0, *pred_pull(protos, raws, top, total, pull), outs, flipped)


def target_kernel(info, codes, preds, near, across, offset, *refs):
    *refs, total, pull, flipped = refs
    earlier, outs = refs[: len(refs) // 2], refs[len(refs) // 2 :]
    total[...] = jnp.zeros(total.shape, jnp.float32)
    pull[...] = jnp.zeros(pull.shape, jnp.float32)
    over_chunks(
        (near, across),
        offset.shape[2],
        lambda j, part: target_step(codes, part, offset, total, pull, j),
        True,
    )
    send(info, 0, pull[...], target_stats(preds, total, pull), outs, flipped)
    for part, out in zip(earlier, outs):
        out[part.shape[0] :, :] = part[...]


def both_kernel(proto_count, info, *refs):
    near, across, offset = refs[2 * proto_count : 2 * proto_count + 3]
    outs = refs[2 * proto_count + 3 : -10]
    raws, top, total, pull, flipped, codes, preds, held, pull_pred, total_pred = refs[-10:]
    protos = near, across
    placed_rows(info, refs[:proto_count], codes)
    placed_rows(info, refs[proto_count : 2 * proto_count], preds)
    top[...] = jnp.full(top.shape, low, jnp.float32)
    total[...] = jnp.zeros(total.shape, jnp.float32)
    pull[...] = jnp.zeros(pull.shape, jnp.float32)

    def step(j, part):
        pred_logits(preds, part, raws, top, j)
        held[j] = bare(target_values(codes, part, offset, total, j))

    def beside(j, part):
        pull[...] += jnp.dot(held[j], part, preferred_element_type=jnp.float32)

    over_chunks(protos, offset.shape[2], step)
    done = pred_pull(protos, raws, top, total_pred, pull_pred, beside)
    send(info, 0, pull[...], target_stats(preds, total, pull), outs, flipped)
    send(info, 1, *done, outs, flipped)


def rows_part(info, codes, preds, protos, offset, rows, proto_count, away, earlier):
    count, dim = protos[0].shape
    share = dim // proto_count
    width = min(chunk, count)
    shapes = [(2 * count // width, rows, width), (rows, 128), (rows, 128), (rows, dim), (dim, rows)]
    scratch = [pltpu.VMEM(shape, jnp.float32) for shape in shapes]
    if codes is None:
        kernel, ins, passed = pred_kernel, [preds, *protos], (1, 2)
        specs = [whole(value) for value in ins]
    elif not away:
        kernel, ins, passed = target_kernel, [codes, preds, *protos, offset, *earlier], ()
        specs, scratch = [whole(value) for value in ins], scratch[2:]
    else:
        kernel, ins = functools.partial(both_kernel, proto_count), [*codes, *preds, *protos, offset]
        passed = tuple(2 * proto_count + i for i in range(2))
        quarter = pl.BlockSpec((1, *codes[0].shape[1:]), lambda i, info: (away - 1, 0, 0))
        specs = [quarter] * (2 * proto_count) + [whole(value) for value in ins[-3:]]
        scratch = [*scratch] + [pltpu.VMEM((rows, dim), jnp.bfloat16)] * 2
        scratch += [pltpu.VMEM(shapes[0], jnp.bfloat16)]
        scratch += [pltpu.VMEM(shape, jnp.float32) for shape in ((rows, dim), (rows, 128))]
    parts, work = 2 if codes is not None else 1, 2 if away else 1
    high, tall = parts * (share + stat_rows), parts * (share + sent_rows)
    outs = [jax.ShapeDtypeStruct((high, rows), jnp.float32)]
    outs += [jax.ShapeDtypeStruct((tall, rows), jnp.bfloat16)] * (proto_count - 1)
    return call(
        kernel, "rows_part", info, (1,), ins, specs, outs, [whole(out) for out in outs], scratch,
        work * 8 * rows * count * dim, work * 2 * rows * count,
        20 if kernel is target_kernel else 36, passed,
    )


names = ["target", "pred"]


def packed_far(target, pred):
    pull, stats = pred
    high = bare(pull)
    rest = bare(pull - high.astype(jnp.float32))
    return jnp.concatenate([bare(target[0]), high, rest, split_stats([*target[1], *stats])], axis=0)


def parted_far(value):
    share = (value.shape[0] - sent_rows) // 3
    target, high, rest = [
        value[i * share : (i + 1) * share, :].astype(jnp.float32) for i in range(3)
    ]
    stats = join_stats(value[3 * share :, :], 4)
    return {"target": (target, stats[:2]), "pred": (high + rest, stats[2:])}


def joined(parts, others=()):
    kept, *sent = parts
    high, tall = kept.shape[0] // len(names), sent[0].shape[0] // len(names)
    return [
        joins[name](
            [parted(kept[i * high : (i + 1) * high, :])]
            + [parted_sent(part[i * tall : (i + 1) * tall, :]) for part in sent]
            + [part[name] for part in others]
        )
        for i, name in enumerate(names)
    ]


def spread_kernel(info, *refs):
    *parts, out = refs
    out[...] = packed_far(*joined(parts))


def join_spread(info, parts):
    high, rows = parts[0].shape
    share = high // len(names) - stat_rows
    out = jax.ShapeDtypeStruct((3 * share + sent_rows, rows), jnp.bfloat16)
    return call(
        spread_kernel, "join_spread", info, (1,), parts, [whole(part) for part in parts], [out],
        [whole(out)], [], 1 << 20, 0, 5,
    )


def final_kernel(count, info, *refs):
    parts, far, (loss, pull) = refs[:count], refs[count:-2], refs[-2:]
    far = [parted_far(part[...]) for part in far]
    (target, (mass, cross)), (pred, (peak, total)) = joined(parts, far)
    pull[...] = target / mass - pred / total
    loss[...] = peak * log2 + jnp.log(total) - cross / mass / pred_temp


def finish(info, own, others):
    high, length = own[0].shape
    outs = [
        jax.ShapeDtypeStruct((1, length), jnp.float32),
        jax.ShapeDtypeStruct((high // len(names) - stat_rows, length), jnp.float32),
    ]
    ins = [*own, *others]
    return call(
        functools.partial(final_kernel, len(own)), "finish", info, (1,), ins,
        [whole(value) for value in ins], outs, [whole(out) for out in outs], [], 1 << 20, 0, 5,
    )[1:]


def swap(value, axis, bits):
    count = lax.axis_size(axis)
    return lax.ppermute(value, axis, [(i, i ^ bits) for i in range(count)])


def body(codes_view, pred_view, prototypes):
    rows = codes_view.shape[0]
    dp_count, proto_count = lax.axis_size("dp"), lax.axis_size("proto")
    z_count = dp_count // 2
    me, proto = lax.axis_index("dp"), lax.axis_index("proto")
    info = jnp.stack([me // 2, proto]).astype(jnp.int32)

    def sent(values):
        return [values[0]] + [swap(value, "proto", s) for s, value in enumerate(values[1:], 1)]

    protos = prototypes, swap(prototypes, "dp", 1)
    part = rows // proto_count
    piece = jnp.concatenate(
        [
            lax.dynamic_slice_in_dim(view, proto * part, part, 0)
            for view in (codes_view, pred_view)
        ]
    )
    quarters = [swap(piece, "dp", 2 * t) for t in range(1, z_count)]

    def around(value):
        return [value] + [swap(value, "proto", s) for s in range(1, proto_count)]

    info, stats, *protos = stats_part(info, [codes_view], protos, None)
    info, *values = rows_part(info, None, pred_view, protos, None, rows, proto_count, 0, None)
    *earlier, near, across = values
    quarters, info = lax.optimization_barrier((quarters, info))
    codes = around(jnp.stack([value[:part] for value in quarters]))
    preds = jnp.stack([value[part:] for value in quarters])
    info, stats, *protos = stats_part(info, codes[:1], (near, across), stats)
    preds, info = lax.optimization_barrier((preds, info))
    preds = around(preds)
    info, stats, *protos = stats_part(info, codes[1:], protos, stats)
    info, offset = offset_part(info, stats, swap(stats, "dp", 1))

    far, waiting = [], []
    for away in range(z_count - 1, 0, -1):
        info, *values = rows_part(
            info, codes, preds, protos, offset, rows, proto_count, away, None
        )
        *out, near, across = values
        protos = near, across
        out = sent(out)
        for past, arrived in waiting:
            if far:
                far, arrived = lax.optimization_barrier((far, arrived))
            info, part = join_spread(info, arrived)
            far.append(swap(part, "dp", 2 * past))
        waiting = [(away, out)]
    info, *out = rows_part(
        info, codes_view, pred_view, protos, offset, rows, proto_count, 0, earlier
    )
    own = sent(out)
    ((past, arrived),) = waiting
    far, arrived = lax.optimization_barrier((far, arrived))
    info, part = join_spread(info, arrived)
    loss, pull = finish(info, own, [*far, swap(part, "dp", 2 * past)])
    return (loss.reshape(rows), pull.T)


def solution(mesh):
    placed = (P("dp", None), P("dp", None), P(("proto", "dp"), None))
    return jax.shard_map(
        body, mesh=mesh, in_specs=placed, out_specs=(P("dp"), P("dp", "proto")), check_vma=False
    )
```

```python
import functools
import math

import jax
import jax.numpy as jnp
from jax import lax
from jax.experimental import pallas as pl
from jax.experimental.pallas import tpu as pltpu
from jax.sharding import PartitionSpec as P

code_temp = 0.05
pred_temp = 0.1
code_scale = math.log2(math.e) / code_temp
pred_scale = math.log2(math.e) / pred_temp
log2 = math.log(2.0)
too_large = 2.0**100
stat_rows = 8
sent_rows = 16
low = -1e30
chunk = 1024
mebi = 1024 * 1024


def scores(embeds, protos):
    return lax.dot_general(
        embeds, protos, (((1,), (1,)), ((), ())), preferred_element_type=jnp.float32
    )


def bare(value):
    return value.astype(jnp.bfloat16)


def add(parts):
    return functools.reduce(jnp.add, parts)


def lane_fold(combine, value):
    parts = [value[:, i : i + 128] for i in range(0, value.shape[1], 128)]
    return functools.reduce(combine, parts)


def padded(rows, width):
    filler = jnp.zeros((stat_rows - len(rows), width), jnp.float32)
    return jnp.concatenate([*rows, filler], axis=0)


def split_stats(stats):
    terms = []
    for row in stats:
        for _ in range(3):
            term = bare(row)
            row = row - term.astype(jnp.float32)
            terms.append(term)
    filler = jnp.zeros((sent_rows - len(terms), stats[0].shape[1]), jnp.bfloat16)
    return jnp.concatenate([*terms, filler], axis=0)


def join_stats(terms, count):
    wide = terms.astype(jnp.float32)
    return [add([wide[3 * i + j : 3 * i + j + 1] for j in range(3)]) for i in range(count)]


def parted(value):
    share = value.shape[0] - stat_rows
    return value[:share, :], [value[share + i : share + i + 1, :] for i in range(2)]


def parted_sent(value):
    share = value.shape[0] - sent_rows
    return value[:share, :].astype(jnp.float32), join_stats(value[share:, :], 2)


def packed(part):
    pull, stats = part
    return jnp.concatenate([pull, padded(stats, pull.shape[1])], axis=0)


def join_preds(parts):
    peak = functools.reduce(jnp.maximum, [stats[0] for _, stats in parts])
    factors = [jnp.exp2(stats[0] - peak) for _, stats in parts]
    pull = add([part * factor for (part, _), factor in zip(parts, factors)])
    total = add([stats[1] * factor for (_, stats), factor in zip(parts, factors)])
    return pull, [peak, total]


def join_targets(parts):
    stats = [add([stats[i] for _, stats in parts]) for i in range(2)]
    return add([part for part, _ in parts]), stats


joins = {"pred": join_preds, "target": join_targets}


def send(info, place, pull, stats, outs, flipped):
    kept, *sent = outs
    share = pull.shape[1] // len(outs)
    high, tall = share + stat_rows, share + sent_rows
    flipped[...] = pull.T
    mine = pl.multiple_of(info[1] * share, share)
    kept[place * high : place * high + share, :] = flipped[pl.ds(mine, share), :]
    kept[place * high + share : (place + 1) * high, :] = padded(stats, pull.shape[0])
    terms = split_stats(stats)
    for s, out in enumerate(sent, 1):
        start = pl.multiple_of((info[1] ^ s) * share, share)
        out[place * tall : place * tall + share, :] = bare(flipped[pl.ds(start, share), :])
        out[place * tall + share : (place + 1) * tall, :] = terms


def whole(value):
    return pl.BlockSpec(value.shape, lambda *_: (0,) * len(value.shape))


def call(kernel, name, info, grid, ins, in_specs, outs, out_specs, scratch, flops, exps, room, passed=()):
    count, total = len(ins), len(ins) + len(outs)

    def without(*refs):
        return kernel(*refs[: 1 + total], *refs[1 + total + len(passed) :])

    outs = [*outs, *[jax.ShapeDtypeStruct(ins[i].shape, ins[i].dtype) for i in passed]]
    out_specs = [*out_specs, *[pl.BlockSpec(memory_space=pl.ANY)] * len(passed)]
    values = pl.pallas_call(
        without,
        grid_spec=pltpu.PrefetchScalarGridSpec(
            num_scalar_prefetch=1,
            grid=grid,
            in_specs=in_specs,
            out_specs=out_specs,
            scratch_shapes=scratch,
        ),
        out_shape=outs,
        input_output_aliases={1 + i: total - count + k for k, i in enumerate(passed)},
        compiler_params=pltpu.CompilerParams(vmem_limit_bytes=room * mebi),
        cost_estimate=pl.CostEstimate(flops=flops, bytes_accessed=flops // 128, transcendentals=exps),
        name=name,
    )(info, *ins)
    info, first = lax.optimization_barrier((info, values[0]))
    return info, first, *values[1:]


def placed_rows(info, quarters, block):
    part = quarters[0].shape[1]
    for s, quarter in enumerate(quarters):
        place = pl.multiple_of((info[1] ^ s) * part, part)
        block[pl.ds(place, part), :] = quarter[0]


def over_chunks(protos, width, step, unrolled=False):
    count = protos[0].shape[0] // width
    if unrolled:
        for i in range(count):
            for half, part in enumerate(protos):
                step(half * count + i, part[i * width : (i + 1) * width, :])
        return

    def both(i, carry):
        at = pl.ds(pl.multiple_of(i * width, width), width)
        for half, part in enumerate(protos):
            step(half * count + i, part[at, :])
        return carry

    lax.fori_loop(0, count, both, 0)


def column_sums(raw, peak):
    return jnp.sum(jnp.exp2((raw - peak) * code_scale), axis=0, keepdims=True)


def stats_kernel(fresh, info, *refs):
    if fresh:
        *codes, near, across, stats, copied = refs
        copied[...] = near[...]
    else:
        *codes, near, across, before, stats = refs
        stats[...] = before[...]
    protos, width = (near, across), stats.shape[2]

    def first(j, part):
        raw = scores(codes[0][...], part)
        peak = jnp.max(raw, axis=0, keepdims=True)
        stats[j, 0:1, :] = peak
        stats[j, 1:2, :] = column_sums(raw, peak)

    def kept_peak(rows, j, part):
        stats[j, 1:2, :] += column_sums(scores(rows, part), stats[j, 0:1, :])

    def new_peak(rows, j, part):
        raw = scores(rows, part)
        old, total = stats[j, 0:1, :], stats[j, 1:2, :]
        peak = jnp.maximum(old, jnp.max(raw, axis=0, keepdims=True))
        stats[j, 0:1, :] = peak
        stats[j, 1:2, :] = total * jnp.exp2((old - peak) * code_scale) + column_sums(raw, peak)

    def all_rows(add_rows, unrolled):
        for part in codes:
            rows = part[...].reshape(-1, part.shape[-1])
            over_chunks(protos, width, functools.partial(add_rows, rows), unrolled)

    if fresh:
        over_chunks(protos, width, first, True)
        return
    all_rows(kept_peak, True)
    worst = jnp.max(stats[:, 1:2, :])

    @pl.when(jnp.logical_not(worst < too_large))
    def _():
        stats[...] = before[...]
        all_rows(new_peak, False)


def stats_part(info, codes, protos, before):
    count, dim = protos[0].shape
    width = min(chunk, count)
    rows = sum(math.prod(part.shape[:-1]) for part in codes)
    outs = [jax.ShapeDtypeStruct((2 * count // width, stat_rows, width), jnp.float32)]
    ins, passed = [*codes, *protos], [len(codes), len(codes) + 1]
    if before is None:
        outs.append(jax.ShapeDtypeStruct(protos[0].shape, protos[0].dtype))
        passed = passed[1:]
    else:
        ins.append(before)
    return call(
        functools.partial(stats_kernel, before is None), "stats_part", info, (1,), ins,
        [whole(value) for value in ins], outs, [whole(out) for out in outs], [],
        4 * rows * count * dim, 2 * rows * count, 12, passed,
    )


def offset_kernel(info, stats, other, out):
    count = stats.shape[0] // 2
    for j in range(2 * count):
        here, there = stats[j], other[(j + count) % (2 * count)]
        peak = jnp.maximum(here[0:1], there[0:1])
        mass = here[1:2] * jnp.exp2((here[0:1] - peak) * code_scale) + there[1:2] * jnp.exp2(
            (there[0:1] - peak) * code_scale
        )
        offset = peak * code_scale + jnp.log2(mass)
        out[j] = jnp.broadcast_to(offset, out.shape[1:])


def offset_part(info, stats, other):
    return call(
        offset_kernel, "offset_part", info, (1,), [stats, other], [whole(stats)] * 2, [stats],
        [whole(stats)], [], 1 << 20, 0, 5,
    )


def weighted(value, protos):
    return jnp.dot(bare(value), protos, preferred_element_type=jnp.float32)


def row_of(combine, value):
    return combine(value.T, axis=0, keepdims=True)


def pred_logits(preds, protos, raws, top, j):
    raw = scores(preds[...], protos)
    raws[j] = raw
    top[...] = jnp.maximum(top[...], lane_fold(jnp.maximum, raw))


def pred_pull(protos, raws, top, total, pull, beside=None):
    width = raws.shape[2]
    stats = [row_of(jnp.max, top[...]) * pred_scale]
    peak = jnp.max(top[...], axis=1, keepdims=True)
    top[...] = jnp.broadcast_to(peak, top.shape)
    total[...] = jnp.zeros(total.shape, jnp.float32)
    pull[...] = jnp.zeros(pull.shape, jnp.float32)

    def step(j, protos):
        peak = jnp.concatenate([top[...]] * (width // 128), axis=1)
        value = jnp.exp2((raws[j] - peak) * pred_scale)
        total[...] += lane_fold(jnp.add, value)
        pull[...] += weighted(value, protos)
        if beside is not None:
            beside(j, protos)

    over_chunks(protos, width, step)
    return pull[...], [*stats, row_of(jnp.sum, total[...])]


def target_values(codes, protos, offset, total, j):
    value = jnp.exp2(scores(codes[...], protos) * code_scale - offset[j, 0:1, :])
    total[...] += lane_fold(jnp.add, value)
    return value


def target_step(codes, protos, offset, total, pull, j):
    pull[...] += weighted(target_values(codes, protos, offset, total, j), protos)


def target_stats(preds, total, pull):
    cross = lane_fold(jnp.add, pull[...] * preds[...].astype(jnp.float32))
    return [row_of(jnp.sum, total[...]), row_of(jnp.sum, cross)]


def pred_kernel(info, preds, near, across, *refs):
    *outs, raws, top, total, pull, flipped = refs
    protos = near, across
    top[...] = jnp.full(top.shape, low, jnp.float32)
    over_chunks(protos, raws.shape[2], lambda j, part: pred_logits(preds, part, raws, top, j))
    send(info, 0, *pred_pull(protos, raws, top, total, pull), outs, flipped)


def target_kernel(info, codes, preds, near, across, offset, *refs):
    *refs, total, pull, flipped = refs
    earlier, outs = refs[: len(refs) // 2], refs[len(refs) // 2 :]
    total[...] = jnp.zeros(total.shape, jnp.float32)
    pull[...] = jnp.zeros(pull.shape, jnp.float32)
    over_chunks(
        (near, across),
        offset.shape[2],
        lambda j, part: target_step(codes, part, offset, total, pull, j),
        True,
    )
    send(info, 0, pull[...], target_stats(preds, total, pull), outs, flipped)
    for part, out in zip(earlier, outs):
        out[part.shape[0] :, :] = part[...]


def both_kernel(proto_count, info, *refs):
    near, across, offset = refs[2 * proto_count : 2 * proto_count + 3]
    outs = refs[2 * proto_count + 3 : -10]
    raws, top, total, pull, flipped, codes, preds, held, pull_pred, total_pred = refs[-10:]
    protos = near, across
    placed_rows(info, refs[:proto_count], codes)
    placed_rows(info, refs[proto_count : 2 * proto_count], preds)
    top[...] = jnp.full(top.shape, low, jnp.float32)
    total[...] = jnp.zeros(total.shape, jnp.float32)
    pull[...] = jnp.zeros(pull.shape, jnp.float32)

    def step(j, part):
        pred_logits(preds, part, raws, top, j)
        held[j] = bare(target_values(codes, part, offset, total, j))

    def beside(j, part):
        pull[...] += jnp.dot(held[j], part, preferred_element_type=jnp.float32)

    over_chunks(protos, offset.shape[2], step)
    done = pred_pull(protos, raws, top, total_pred, pull_pred, beside)
    send(info, 0, pull[...], target_stats(preds, total, pull), outs, flipped)
    send(info, 1, *done, outs, flipped)


def rows_part(info, codes, preds, protos, offset, rows, proto_count, away, earlier):
    count, dim = protos[0].shape
    share = dim // proto_count
    width = min(chunk, count)
    shapes = [(2 * count // width, rows, width), (rows, 128), (rows, 128), (rows, dim), (dim, rows)]
    scratch = [pltpu.VMEM(shape, jnp.float32) for shape in shapes]
    if codes is None:
        kernel, ins, passed = pred_kernel, [preds, *protos], (1, 2)
        specs = [whole(value) for value in ins]
    elif not away:
        kernel, ins, passed = target_kernel, [codes, preds, *protos, offset, *earlier], ()
        specs, scratch = [whole(value) for value in ins], scratch[2:]
    else:
        kernel, ins = functools.partial(both_kernel, proto_count), [*codes, *preds, *protos, offset]
        passed = tuple(2 * proto_count + i for i in range(2))
        quarter = pl.BlockSpec((1, *codes[0].shape[1:]), lambda i, info: (away - 1, 0, 0))
        specs = [quarter] * (2 * proto_count) + [whole(value) for value in ins[-3:]]
        scratch = [*scratch] + [pltpu.VMEM((rows, dim), jnp.bfloat16)] * 2
        scratch += [pltpu.VMEM(shapes[0], jnp.bfloat16)]
        scratch += [pltpu.VMEM(shape, jnp.float32) for shape in ((rows, dim), (rows, 128))]
    parts, work = 2 if codes is not None else 1, 2 if away else 1
    high, tall = parts * (share + stat_rows), parts * (share + sent_rows)
    outs = [jax.ShapeDtypeStruct((high, rows), jnp.float32)]
    outs += [jax.ShapeDtypeStruct((tall, rows), jnp.bfloat16)] * (proto_count - 1)
    return call(
        kernel, "rows_part", info, (1,), ins, specs, outs, [whole(out) for out in outs], scratch,
        work * 8 * rows * count * dim, work * 2 * rows * count,
        12 if kernel is target_kernel else 26, passed,
    )


names = ["target", "pred"]


def packed_far(target, pred):
    pull, stats = pred
    high = bare(pull)
    rest = bare(pull - high.astype(jnp.float32))
    return jnp.concatenate([bare(target[0]), high, rest, split_stats([*target[1], *stats])], axis=0)


def parted_far(value):
    share = (value.shape[0] - sent_rows) // 3
    target, high, rest = [
        value[i * share : (i + 1) * share, :].astype(jnp.float32) for i in range(3)
    ]
    stats = join_stats(value[3 * share :, :], 4)
    return {"target": (target, stats[:2]), "pred": (high + rest, stats[2:])}


def joined(parts, others=()):
    kept, *sent = parts
    high, tall = kept.shape[0] // len(names), sent[0].shape[0] // len(names)
    return [
        joins[name](
            [parted(kept[i * high : (i + 1) * high, :])]
            + [parted_sent(part[i * tall : (i + 1) * tall, :]) for part in sent]
            + [part[name] for part in others]
        )
        for i, name in enumerate(names)
    ]


def spread_kernel(info, *refs):
    *parts, out = refs
    out[...] = packed_far(*joined(parts))


def join_spread(info, parts):
    high, rows = parts[0].shape
    share = high // len(names) - stat_rows
    out = jax.ShapeDtypeStruct((3 * share + sent_rows, rows), jnp.bfloat16)
    return call(
        spread_kernel, "join_spread", info, (1,), parts, [whole(part) for part in parts], [out],
        [whole(out)], [], 1 << 20, 0, 5,
    )


def final_kernel(count, info, *refs):
    parts, far, (loss, pull) = refs[:count], refs[count:-2], refs[-2:]
    far = [parted_far(part[...]) for part in far]
    (target, (mass, cross)), (pred, (peak, total)) = joined(parts, far)
    pull[...] = target / mass - pred / total
    loss[...] = peak * log2 + jnp.log(total) - cross / mass / pred_temp


def finish(info, own, others):
    high, length = own[0].shape
    outs = [
        jax.ShapeDtypeStruct((1, length), jnp.float32),
        jax.ShapeDtypeStruct((high // len(names) - stat_rows, length), jnp.float32),
    ]
    ins = [*own, *others]
    return call(
        functools.partial(final_kernel, len(own)), "finish", info, (1,), ins,
        [whole(value) for value in ins], outs, [whole(out) for out in outs], [], 1 << 20, 0, 5,
    )[1:]


def swap(value, axis, bits):
    count = lax.axis_size(axis)
    return lax.ppermute(value, axis, [(i, i ^ bits) for i in range(count)])


def body(codes_view, pred_view, prototypes):
    rows = codes_view.shape[0]
    dp_count, proto_count = lax.axis_size("dp"), lax.axis_size("proto")
    z_count = dp_count // 2
    me, proto = lax.axis_index("dp"), lax.axis_index("proto")
    info = jnp.stack([me // 2, proto]).astype(jnp.int32)

    def sent(values):
        return [values[0]] + [swap(value, "proto", s) for s, value in enumerate(values[1:], 1)]

    protos = prototypes, swap(prototypes, "dp", 1)
    part = rows // proto_count
    piece = jnp.concatenate(
        [
            lax.dynamic_slice_in_dim(view, proto * part, part, 0)
            for view in (codes_view, pred_view)
        ]
    )
    quarters = [swap(piece, "dp", 2 * t) for t in range(1, z_count)]

    def around(value):
        return [value] + [swap(value, "proto", s) for s in range(1, proto_count)]

    info, stats, *protos = stats_part(info, [codes_view], protos, None)
    info, *values = rows_part(info, None, pred_view, protos, None, rows, proto_count, 0, None)
    *earlier, near, across = values
    quarters, info = lax.optimization_barrier((quarters, info))
    codes = around(jnp.stack([value[:part] for value in quarters]))
    preds = jnp.stack([value[part:] for value in quarters])
    info, stats, *protos = stats_part(info, codes[:1], (near, across), stats)
    preds, info = lax.optimization_barrier((preds, info))
    preds = around(preds)
    info, stats, *protos = stats_part(info, codes[1:], protos, stats)
    info, offset = offset_part(info, stats, swap(stats, "dp", 1))

    far, waiting = [], []
    for away in range(z_count - 1, 0, -1):
        info, *values = rows_part(
            info, codes, preds, protos, offset, rows, proto_count, away, None
        )
        *out, near, across = values
        protos = near, across
        out = sent(out)
        for past, arrived in waiting:
            if far:
                far, arrived = lax.optimization_barrier((far, arrived))
            info, part = join_spread(info, arrived)
            far.append(swap(part, "dp", 2 * past))
        waiting = [(away, out)]
    info, *out = rows_part(
        info, codes_view, pred_view, protos, offset, rows, proto_count, 0, earlier
    )
    own = sent(out)
    ((past, arrived),) = waiting
    far, arrived = lax.optimization_barrier((far, arrived))
    info, part = join_spread(info, arrived)
    loss, pull = finish(info, own, [*far, swap(part, "dp", 2 * past)])
    return (loss.reshape(rows), pull.T)


def solution(mesh):
    placed = (P("dp", None), P("dp", None), P(("proto", "dp"), None))
    return jax.shard_map(
        body, mesh=mesh, in_specs=placed, out_specs=(P("dp"), P("dp", "proto")), check_vma=False
    )
```

```python
import functools
import math

import jax
import jax.numpy as jnp
from jax import lax
from jax.experimental import pallas as pl
from jax.experimental.pallas import tpu as pltpu
from jax.sharding import PartitionSpec as P

code_temp = 0.05
pred_temp = 0.1
code_scale = math.log2(math.e) / code_temp
pred_scale = math.log2(math.e) / pred_temp
log2 = math.log(2.0)
too_large = 2.0**100
stat_rows = 8
sent_rows = 16
low = -1e30
chunk = 1024
mebi = 1024 * 1024


def scores(embeds, protos):
    return lax.dot_general(
        embeds, protos, (((1,), (1,)), ((), ())), preferred_element_type=jnp.float32
    )


def bare(value):
    return value.astype(jnp.bfloat16)


def add(parts):
    return functools.reduce(jnp.add, parts)


def lane_fold(combine, value):
    parts = [value[:, i : i + 128] for i in range(0, value.shape[1], 128)]
    return functools.reduce(combine, parts)


def padded(rows, width):
    filler = jnp.zeros((stat_rows - len(rows), width), jnp.float32)
    return jnp.concatenate([*rows, filler], axis=0)


def split_stats(stats):
    terms = []
    for row in stats:
        for _ in range(3):
            term = bare(row)
            row = row - term.astype(jnp.float32)
            terms.append(term)
    filler = jnp.zeros((sent_rows - len(terms), stats[0].shape[1]), jnp.bfloat16)
    return jnp.concatenate([*terms, filler], axis=0)


def join_stats(terms, count):
    wide = terms.astype(jnp.float32)
    return [add([wide[3 * i + j : 3 * i + j + 1] for j in range(3)]) for i in range(count)]


def parted(value):
    share = value.shape[0] - stat_rows
    return value[:share, :], [value[share + i : share + i + 1, :] for i in range(2)]


def parted_sent(value):
    share = value.shape[0] - sent_rows
    return value[:share, :].astype(jnp.float32), join_stats(value[share:, :], 2)


def packed(part):
    pull, stats = part
    return jnp.concatenate([pull, padded(stats, pull.shape[1])], axis=0)


def join_preds(parts):
    peak = functools.reduce(jnp.maximum, [stats[0] for _, stats in parts])
    factors = [jnp.exp2(stats[0] - peak) for _, stats in parts]
    pull = add([part * factor for (part, _), factor in zip(parts, factors)])
    total = add([stats[1] * factor for (_, stats), factor in zip(parts, factors)])
    return pull, [peak, total]


def join_targets(parts):
    stats = [add([stats[i] for _, stats in parts]) for i in range(2)]
    return add([part for part, _ in parts]), stats


joins = {"pred": join_preds, "target": join_targets}


def send(info, place, pull, stats, outs, flipped):
    kept, *sent = outs
    share = pull.shape[1] // len(outs)
    high, tall = share + stat_rows, share + sent_rows
    flipped[...] = pull.T
    mine = pl.multiple_of(info[1] * share, share)
    kept[place * high : place * high + share, :] = flipped[pl.ds(mine, share), :]
    kept[place * high + share : (place + 1) * high, :] = padded(stats, pull.shape[0])
    terms = split_stats(stats)
    for s, out in enumerate(sent, 1):
        start = pl.multiple_of((info[1] ^ s) * share, share)
        out[place * tall : place * tall + share, :] = bare(flipped[pl.ds(start, share), :])
        out[place * tall + share : (place + 1) * tall, :] = terms


def whole(value):
    return pl.BlockSpec(value.shape, lambda *_: (0,) * len(value.shape))


def call(kernel, name, info, grid, ins, in_specs, outs, out_specs, scratch, flops, exps, room, passed=()):
    count, total = len(ins), len(ins) + len(outs)

    def without(*refs):
        return kernel(*refs[: 1 + total], *refs[1 + total + len(passed) :])

    outs = [*outs, *[jax.ShapeDtypeStruct(ins[i].shape, ins[i].dtype) for i in passed]]
    out_specs = [*out_specs, *[pl.BlockSpec(memory_space=pl.ANY)] * len(passed)]
    values = pl.pallas_call(
        without,
        grid_spec=pltpu.PrefetchScalarGridSpec(
            num_scalar_prefetch=1,
            grid=grid,
            in_specs=in_specs,
            out_specs=out_specs,
            scratch_shapes=scratch,
        ),
        out_shape=outs,
        input_output_aliases={1 + i: total - count + k for k, i in enumerate(passed)},
        compiler_params=pltpu.CompilerParams(vmem_limit_bytes=room * mebi),
        cost_estimate=pl.CostEstimate(flops=flops, bytes_accessed=flops // 128, transcendentals=exps),
        name=name,
    )(info, *ins)
    info, first = lax.optimization_barrier((info, values[0]))
    return info, first, *values[1:]


def placed_rows(info, quarters, block):
    part = quarters[0].shape[1]
    for s, quarter in enumerate(quarters):
        place = pl.multiple_of((info[1] ^ s) * part, part)
        block[pl.ds(place, part), :] = quarter[0]


def over_chunks(protos, width, step, unrolled=False):
    count = protos[0].shape[0] // width
    if unrolled:
        for i in range(count):
            for half, part in enumerate(protos):
                step(half * count + i, part[i * width : (i + 1) * width, :])
        return

    def both(i, carry):
        at = pl.ds(pl.multiple_of(i * width, width), width)
        for half, part in enumerate(protos):
            step(half * count + i, part[at, :])
        return carry

    lax.fori_loop(0, count, both, 0)


def column_sums(raw, peak):
    return jnp.sum(jnp.exp2((raw - peak) * code_scale), axis=0, keepdims=True)


def stats_kernel(fresh, info, *refs):
    if fresh:
        *codes, near, across, stats, copied = refs
        copied[...] = near[...]
    else:
        *codes, near, across, before, stats = refs
        stats[...] = before[...]
    protos, width = (near, across), stats.shape[2]

    def first(j, part):
        raw = scores(codes[0][...], part)
        peak = jnp.max(raw, axis=0, keepdims=True)
        stats[j, 0:1, :] = peak
        stats[j, 1:2, :] = column_sums(raw, peak)

    def kept_peak(rows, j, part):
        stats[j, 1:2, :] += column_sums(scores(rows, part), stats[j, 0:1, :])

    def new_peak(rows, j, part):
        raw = scores(rows, part)
        old, total = stats[j, 0:1, :], stats[j, 1:2, :]
        peak = jnp.maximum(old, jnp.max(raw, axis=0, keepdims=True))
        stats[j, 0:1, :] = peak
        stats[j, 1:2, :] = total * jnp.exp2((old - peak) * code_scale) + column_sums(raw, peak)

    def all_rows(add_rows, unrolled):
        for part in codes:
            rows = part[...].reshape(-1, part.shape[-1])
            over_chunks(protos, width, functools.partial(add_rows, rows), unrolled)

    if fresh:
        over_chunks(protos, width, first, True)
        return
    all_rows(kept_peak, True)
    worst = jnp.max(stats[:, 1:2, :])

    @pl.when(jnp.logical_not(worst < too_large))
    def _():
        stats[...] = before[...]
        all_rows(new_peak, False)


def stats_part(info, codes, protos, before):
    count, dim = protos[0].shape
    width = min(chunk, count)
    rows = sum(math.prod(part.shape[:-1]) for part in codes)
    outs = [jax.ShapeDtypeStruct((2 * count // width, stat_rows, width), jnp.float32)]
    ins, passed = [*codes, *protos], [len(codes), len(codes) + 1]
    if before is None:
        outs.append(jax.ShapeDtypeStruct(protos[0].shape, protos[0].dtype))
        passed = passed[1:]
    else:
        ins.append(before)
    return call(
        functools.partial(stats_kernel, before is None), "stats_part", info, (1,), ins,
        [whole(value) for value in ins], outs, [whole(out) for out in outs], [],
        4 * rows * count * dim, 2 * rows * count, 12, passed,
    )


def offset_kernel(info, stats, other, out):
    count = stats.shape[0] // 2
    for j in range(2 * count):
        here, there = stats[j], other[(j + count) % (2 * count)]
        peak = jnp.maximum(here[0:1], there[0:1])
        mass = here[1:2] * jnp.exp2((here[0:1] - peak) * code_scale) + there[1:2] * jnp.exp2(
            (there[0:1] - peak) * code_scale
        )
        offset = peak * code_scale + jnp.log2(mass)
        out[j] = jnp.broadcast_to(offset, out.shape[1:])


def offset_part(info, stats, other):
    return call(
        offset_kernel, "offset_part", info, (1,), [stats, other], [whole(stats)] * 2, [stats],
        [whole(stats)], [], 1 << 20, 0, 5,
    )


def weighted(value, protos):
    return jnp.dot(bare(value), protos, preferred_element_type=jnp.float32)


def row_of(combine, value):
    return combine(value.T, axis=0, keepdims=True)


def pred_logits(preds, protos, raws, top, j):
    raw = scores(preds[...], protos)
    raws[j] = raw
    top[...] = jnp.maximum(top[...], lane_fold(jnp.maximum, raw))


def pred_pull(protos, raws, top, total, pull, beside=None):
    width = raws.shape[2]
    stats = [row_of(jnp.max, top[...]) * pred_scale]
    peak = jnp.max(top[...], axis=1, keepdims=True)
    top[...] = jnp.broadcast_to(peak, top.shape)
    total[...] = jnp.zeros(total.shape, jnp.float32)
    pull[...] = jnp.zeros(pull.shape, jnp.float32)

    def step(j, protos):
        peak = jnp.concatenate([top[...]] * (width // 128), axis=1)
        value = jnp.exp2((raws[j] - peak) * pred_scale)
        total[...] += lane_fold(jnp.add, value)
        pull[...] += weighted(value, protos)
        if beside is not None:
            beside(j, protos)

    over_chunks(protos, width, step)
    return pull[...], [*stats, row_of(jnp.sum, total[...])]


def target_values(codes, protos, offset, total, j):
    value = jnp.exp2(scores(codes[...], protos) * code_scale - offset[j, 0:1, :])
    total[...] += lane_fold(jnp.add, value)
    return value


def target_step(codes, protos, offset, total, pull, j):
    pull[...] += weighted(target_values(codes, protos, offset, total, j), protos)


def target_stats(preds, total, pull):
    cross = lane_fold(jnp.add, pull[...] * preds[...].astype(jnp.float32))
    return [row_of(jnp.sum, total[...]), row_of(jnp.sum, cross)]


def pred_kernel(info, preds, near, across, *refs):
    *outs, raws, top, total, pull, flipped = refs
    protos = near, across
    top[...] = jnp.full(top.shape, low, jnp.float32)
    over_chunks(protos, raws.shape[2], lambda j, part: pred_logits(preds, part, raws, top, j))
    send(info, 0, *pred_pull(protos, raws, top, total, pull), outs, flipped)


def target_kernel(info, codes, preds, near, across, offset, *refs):
    *refs, total, pull, flipped = refs
    earlier, outs = refs[: len(refs) // 2], refs[len(refs) // 2 :]
    total[...] = jnp.zeros(total.shape, jnp.float32)
    pull[...] = jnp.zeros(pull.shape, jnp.float32)
    over_chunks(
        (near, across),
        offset.shape[2],
        lambda j, part: target_step(codes, part, offset, total, pull, j),
        True,
    )
    send(info, 0, pull[...], target_stats(preds, total, pull), outs, flipped)
    for part, out in zip(earlier, outs):
        out[part.shape[0] :, :] = part[...]


def both_kernel(proto_count, info, *refs):
    near, across, offset = refs[2 * proto_count : 2 * proto_count + 3]
    outs = refs[2 * proto_count + 3 : -10]
    raws, top, total, pull, flipped, codes, preds, held, pull_pred, total_pred = refs[-10:]
    protos = near, across
    placed_rows(info, refs[:proto_count], codes)
    placed_rows(info, refs[proto_count : 2 * proto_count], preds)
    top[...] = jnp.full(top.shape, low, jnp.float32)
    total[...] = jnp.zeros(total.shape, jnp.float32)
    pull[...] = jnp.zeros(pull.shape, jnp.float32)

    def step(j, part):
        pred_logits(preds, part, raws, top, j)
        held[j] = bare(target_values(codes, part, offset, total, j))

    def beside(j, part):
        pull[...] += jnp.dot(held[j], part, preferred_element_type=jnp.float32)

    over_chunks(protos, offset.shape[2], step)
    done = pred_pull(protos, raws, top, total_pred, pull_pred, beside)
    send(info, 0, pull[...], target_stats(preds, total, pull), outs, flipped)
    send(info, 1, *done, outs, flipped)


def rows_part(info, codes, preds, protos, offset, rows, proto_count, away, earlier):
    count, dim = protos[0].shape
    share = dim // proto_count
    width = min(chunk, count)
    shapes = [(2 * count // width, rows, width), (rows, 128), (rows, 128), (rows, dim), (dim, rows)]
    scratch = [pltpu.VMEM(shape, jnp.float32) for shape in shapes]
    if codes is None:
        kernel, ins, passed = pred_kernel, [preds, *protos], (1, 2)
        specs = [whole(value) for value in ins]
    elif not away:
        kernel, ins, passed = target_kernel, [codes, preds, *protos, offset, *earlier], ()
        specs, scratch = [whole(value) for value in ins], scratch[2:]
    else:
        kernel, ins = functools.partial(both_kernel, proto_count), [*codes, *preds, *protos, offset]
        passed = tuple(2 * proto_count + i for i in range(2))
        quarter = pl.BlockSpec((1, *codes[0].shape[1:]), lambda i, info: (away - 1, 0, 0))
        specs = [quarter] * (2 * proto_count) + [whole(value) for value in ins[-3:]]
        scratch = [*scratch] + [pltpu.VMEM((rows, dim), jnp.bfloat16)] * 2
        scratch += [pltpu.VMEM(shapes[0], jnp.bfloat16)]
        scratch += [pltpu.VMEM(shape, jnp.float32) for shape in ((rows, dim), (rows, 128))]
    parts, work = 2 if codes is not None else 1, 2 if away else 1
    high, tall = parts * (share + stat_rows), parts * (share + sent_rows)
    outs = [jax.ShapeDtypeStruct((high, rows), jnp.float32)]
    outs += [jax.ShapeDtypeStruct((tall, rows), jnp.bfloat16)] * (proto_count - 1)
    return call(
        kernel, "rows_part", info, (1,), ins, specs, outs, [whole(out) for out in outs], scratch,
        work * 8 * rows * count * dim, work * 2 * rows * count,
        12 if kernel is target_kernel else 26, passed,
    )


names = ["target", "pred"]


def packed_far(target, pred):
    pull, stats = pred
    high = bare(pull)
    rest = bare(pull - high.astype(jnp.float32))
    return jnp.concatenate([bare(target[0]), high, rest, split_stats([*target[1], *stats])], axis=0)


def parted_far(value):
    share = (value.shape[0] - sent_rows) // 3
    target, high, rest = [
        value[i * share : (i + 1) * share, :].astype(jnp.float32) for i in range(3)
    ]
    stats = join_stats(value[3 * share :, :], 4)
    return {"target": (target, stats[:2]), "pred": (high + rest, stats[2:])}


def joined(parts, others=()):
    kept, *sent = parts
    high, tall = kept.shape[0] // len(names), sent[0].shape[0] // len(names)
    return [
        joins[name](
            [parted(kept[i * high : (i + 1) * high, :])]
            + [parted_sent(part[i * tall : (i + 1) * tall, :]) for part in sent]
            + [part[name] for part in others]
        )
        for i, name in enumerate(names)
    ]


def spread_kernel(info, *refs):
    *parts, out = refs
    out[...] = packed_far(*joined(parts))


def join_spread(info, parts):
    high, rows = parts[0].shape
    share = high // len(names) - stat_rows
    out = jax.ShapeDtypeStruct((3 * share + sent_rows, rows), jnp.bfloat16)
    return call(
        spread_kernel, "join_spread", info, (1,), parts, [whole(part) for part in parts], [out],
        [whole(out)], [], 1 << 20, 0, 5,
    )


def final_kernel(count, info, *refs):
    parts, far, (loss, pull) = refs[:count], refs[count:-2], refs[-2:]
    far = [parted_far(part[...]) for part in far]
    (target, (mass, cross)), (pred, (peak, total)) = joined(parts, far)
    pull[...] = target / mass - pred / total
    loss[...] = peak * log2 + jnp.log(total) - cross / mass / pred_temp


def finish(info, own, others):
    high, length = own[0].shape
    outs = [
        jax.ShapeDtypeStruct((1, length), jnp.float32),
        jax.ShapeDtypeStruct((high // len(names) - stat_rows, length), jnp.float32),
    ]
    ins = [*own, *others]
    return call(
        functools.partial(final_kernel, len(own)), "finish", info, (1,), ins,
        [whole(value) for value in ins], outs, [whole(out) for out in outs], [], 1 << 20, 0, 5,
    )[1:]


def swap(value, axis, bits):
    count = lax.axis_size(axis)
    return lax.ppermute(value, axis, [(i, i ^ bits) for i in range(count)])


def body(codes_view, pred_view, prototypes):
    rows = codes_view.shape[0]
    dp_count, proto_count = lax.axis_size("dp"), lax.axis_size("proto")
    z_count = dp_count // 2
    me, proto = lax.axis_index("dp"), lax.axis_index("proto")
    info = jnp.stack([me // 2, proto]).astype(jnp.int32)

    def sent(values):
        return [values[0]] + [swap(value, "proto", s) for s, value in enumerate(values[1:], 1)]

    protos = prototypes, swap(prototypes, "dp", 1)
    part = rows // proto_count
    piece = jnp.concatenate(
        [
            lax.dynamic_slice_in_dim(view, proto * part, part, 0)
            for view in (codes_view, pred_view)
        ]
    )
    quarters = [swap(piece, "dp", 2 * t) for t in range(1, z_count)]

    def around(value):
        return [value] + [swap(value, "proto", s) for s in range(1, proto_count)]

    info, stats, *protos = stats_part(info, [codes_view], protos, None)
    info, *values = rows_part(info, None, pred_view, protos, None, rows, proto_count, 0, None)
    *earlier, near, across = values
    quarters, info = lax.optimization_barrier((quarters, info))
    codes = around(jnp.stack([value[:part] for value in quarters]))
    preds = jnp.stack([value[part:] for value in quarters])
    info, stats, *protos = stats_part(info, codes[:1], (near, across), stats)
    preds, info = lax.optimization_barrier((preds, info))
    preds = around(preds)
    info, stats, *protos = stats_part(info, codes[1:], protos, stats)
    info, offset = offset_part(info, stats, swap(stats, "dp", 1))

    far, waiting = [], []
    for away in range(z_count - 1, 0, -1):
        info, *values = rows_part(
            info, codes, preds, protos, offset, rows, proto_count, away, None
        )
        *out, near, across = values
        protos = near, across
        out = sent(out)
        for past, arrived in waiting:
            if far:
                far, arrived = lax.optimization_barrier((far, arrived))
            info, part = join_spread(info, arrived)
            far.append(swap(part, "dp", 2 * past))
        waiting = [(away, out)]
    info, *out = rows_part(
        info, codes_view, pred_view, protos, offset, rows, proto_count, 0, earlier
    )
    own = sent(out)
    ((past, arrived),) = waiting
    far[:-1], arrived = lax.optimization_barrier((far[:-1], arrived))
    info, part = join_spread(info, arrived)
    loss, pull = finish(info, own, [*far, swap(part, "dp", 2 * past)])
    return (loss.reshape(rows), pull.T)


def solution(mesh):
    placed = (P("dp", None), P("dp", None), P(("proto", "dp"), None))
    return jax.shard_map(
        body, mesh=mesh, in_specs=placed, out_specs=(P("dp"), P("dp", "proto")), check_vma=False
    )
```
